512 devices in a mesh: lat: 8 (over x, core), lev: 8 (over z_lo), obs: 8 (over y, z_hi).
Axes of the slice: x: 4, y: 4, z: 16 (z_hi: 2, z_lo: 8; z = z_hi * 8 + z_lo), core: 2. Of those that a mesh axis runs over, the one named last changes fastest.
Arguments:
- chi: float32 [136, 128, 2048], P('lev', 'lat', 'obs'), may hold values from -6 to 6
- mat_lon: float32 [2048, 2048], P(None, 'obs'), as said below
- mat_lat: float32 [128, 128], P('lat')
- mat_vert: float32 [136, 136], replicated
- chan_table: float32 [616, 136], replicated, may hold values from -0.5 to 0.5
- chan_map: int32 [300], replicated, may hold values from 0 to 615
- error_weight: float32 [300], replicated, may hold values from 0.5 to 2
- innovation: float32 [300, 524288], P(None, ('lat', 'lev', 'obs')), may hold values from -6 to 6
- foot_weight: float32 [4, 524288], P(None, ('lat', 'lev', 'obs')), may hold values from 0.2 to 1
- foot_slot: int32 [4, 524288], P(None, ('lat', 'lev', 'obs')), may hold values from 0 to 4095
- serve_cols: int32 [8, 64, 64, 64], P('lat', ('lev', 'obs')), may hold values from 0 to 511
Outputs:
- gradient: float32 [136, 128, 2048], P('lev', 'lat', 'obs')
The draws below stay inside these ranges and needn't reach their ends.
Inputs may be any that keep to these rules, and one draw needn't show every extreme that they name: mat_lon and mat_lat are symmetric.
All inputs are finite; a program needn't handle non-finite values.
Results may differ from the reference program's by a relative error of at most 0.00015.
Values sent between devices are 32-bit elements; how exact they have to be, the bound alone decides.
No kernel may reach another device: no remote copies, remote signals or barrier semaphores. Data moves between devices by JAX's collectives and lax.ppermute only.
A program may use at most 128 MiB of HBM per device.

```python
import math
import jax
import jax.numpy as jnp
from jax import lax

NLEV = 136
NCH = 300
NTAB = 616
FOOT = 4
CLON = 256
CLAT = 16
OBS_DEV = 1024
NLAT = 128
NLON = 2048
GROUP = 64
COLS_DEV = 512
CAP = 64
OBS_TOTAL = 524288
N_LAT = 8
N_OBS = 8


def kernel_matrix(key, count, span, periodic, symmetric):
    places = jnp.arange(count, dtype=jnp.int32)
    spacing = jnp.abs(places[:, None] - places[None, :])
    if periodic:
        spacing = jnp.minimum(spacing, count - spacing)
    jitter = jax.random.uniform(key, (count, count), jnp.float32)
    if symmetric:
        jitter = 0.5 * (jitter + jitter.T)
    decay = jnp.exp(-spacing.astype(jnp.float32) / span) / jnp.float32(span)
    return jnp.eye(count, dtype=jnp.float32) + decay * (2.0 * jitter)


def draw_mat_lon(key, part):
    key = jax.random.fold_in(key, 11)
    return kernel_matrix(key, NLON, NLON / 2.0, True, True)


def draw_mat_lat(key, part):
    key = jax.random.fold_in(key, 12)
    return kernel_matrix(key, NLAT, NLAT / 2.0, False, True)


def draw_mat_vert(key, part):
    key = jax.random.fold_in(key, 13)
    return kernel_matrix(key, NLEV, 20.0, False, False)


def touch_ends(drawn, rng, low, top_value):
    place = [jax.random.randint(jax.random.fold_in(rng, axis), (), 0, length) for axis, length in enumerate(drawn.shape)]
    main_axis = drawn.shape.index(max(drawn.shape))
    neighbour = place[:main_axis] + [(place[main_axis] + 1) % drawn.shape[main_axis]] + place[main_axis + 1:]
    return drawn.at[tuple(place)].set(low).at[tuple(neighbour)].set(top_value)


def block_levels(rng, dims, cuts, smallest, largest):
    def one(position, shards_of):
        draws = jax.random.uniform(jax.random.fold_in(jax.random.fold_in(rng, 6), position), (shards_of,), jnp.float32, smallest / len(cuts), largest / len(cuts))
        return jnp.repeat(jnp.exp(draws), dims[position] // shards_of).reshape((-1,) + (1,) * (len(dims) - position - 1))

    loudness = one(*cuts[0])
    for cut in cuts[1:]:
        loudness = loudness * one(*cut)
    return loudness


def gaussian(key, shape, spread, limit, shards=(), kind=jnp.bfloat16):
    result = jax.random.normal(key, shape, jnp.float32) * spread
    if len(shards) > 0:
        result = block_levels(key, shape, shards, -0.22, 0.18) * result
    return jnp.clip(result, min=-limit, max=limit).astype(kind)


def setup_inputs(seed: int = 0) -> dict:
    splits = jax.random.split(jax.random.key(seed), 12)
    chi = gaussian(splits[0], (NLEV, NLAT, NLON), 1.0, 6.0, ((0, 8), (1, 8), (2, 8)), jnp.float32)
    mat_lon = draw_mat_lon(jax.random.fold_in(splits[11], 71), 0)
    mat_lat = draw_mat_lat(jax.random.fold_in(splits[11], 71), 0)
    mat_vert = draw_mat_vert(jax.random.fold_in(splits[11], 71), 0)
    chan_table = gaussian(splits[4], (NTAB, NLEV), NLEV ** -0.5, 0.5, (), jnp.float32)
    chan_map = touch_ends(jax.random.randint(splits[5], (NCH,), 0, NTAB), jax.random.fold_in(splits[5], 1), 0, NTAB - 1).astype(jnp.int32)
    error_weight = jnp.clip(jnp.exp(jax.random.uniform(splits[6], (NCH,), jnp.float32, math.log(0.5), math.log(2.0))), 0.5, 2.0)
    innovation = gaussian(splits[7], (NCH, OBS_TOTAL), 1.0, 6.0, ((1, 512),), jnp.float32)
    foot_weight = jnp.clip(0.2 + 0.8 * jax.random.uniform(splits[8], (FOOT, OBS_TOTAL), jnp.float32) ** block_levels(splits[8], (FOOT, OBS_TOTAL), ((1, 512),), -0.2, 0.2), 0.2, 1.0)
    foot_slot = touch_ends(jax.random.randint(splits[9], (FOOT, OBS_TOTAL), 0, GROUP * CAP), jax.random.fold_in(splits[9], 1), 0, (GROUP * CAP) - 1).astype(jnp.int32)
    serve_cols = touch_ends(jax.random.randint(splits[10], (N_LAT, GROUP, GROUP, CAP), 0, COLS_DEV), jax.random.fold_in(splits[10], 1), 0, COLS_DEV - 1).astype(jnp.int32)
    return dict(chi=chi, mat_lon=mat_lon, mat_lat=mat_lat, mat_vert=mat_vert, chan_table=chan_table, chan_map=chan_map, error_weight=error_weight, innovation=innovation, foot_weight=foot_weight, foot_slot=foot_slot, serve_cols=serve_cols)


HIGHEST = lax.Precision.HIGHEST


def apply_lon(field, matrix):
    flat = field.reshape(-1, NLON)
    return jnp.dot(flat, matrix, precision=HIGHEST, preferred_element_type=jnp.float32).reshape(field.shape)


def apply_lat(field, matrix):
    return jnp.einsum("ij,ljk->lik", matrix, field, precision=HIGHEST, preferred_element_type=jnp.float32)


def reference(chi, mat_lon, mat_lat, mat_vert, chan_table, chan_map, error_weight, innovation, foot_weight, foot_slot, serve_cols):
    smoothed = apply_lat(apply_lon(chi, mat_lon), mat_lat)
    profiles = jnp.dot(mat_vert, smoothed.reshape(NLEV, NLAT * NLON), precision=HIGHEST, preferred_element_type=jnp.float32)
    device = (jnp.arange(OBS_TOTAL, dtype=jnp.int32) // OBS_DEV).astype(jnp.int32)
    band = device // GROUP
    viewer = device % GROUP
    owner = (foot_slot // CAP).astype(jnp.int32)
    within = (foot_slot % CAP).astype(jnp.int32)
    local = serve_cols[band[None, :], owner, viewer[None, :], within]
    cell = (owner // N_OBS) * COLS_DEV + local
    row_index = band[None, :] * CLAT + cell // CLON
    lon_index = (owner % N_OBS) * CLON + cell % CLON
    target = (row_index * NLON + lon_index).astype(jnp.int32)
    column_mean = jnp.zeros((NLEV, OBS_TOTAL), jnp.float32)
    for member in range(FOOT):
        column_mean = column_mean + foot_weight[member][None, :] * profiles[:, target[member]]
    matches = (chan_map[:, None] == jnp.arange(NTAB, dtype=jnp.int32)[None, :]).astype(jnp.float32)
    selected = jnp.dot(matches, chan_table, precision=HIGHEST, preferred_element_type=jnp.float32)
    evolved = jnp.dot(selected, column_mean, precision=HIGHEST, preferred_element_type=jnp.float32)
    weighted = error_weight[:, None] * (evolved - innovation)
    pulled = jnp.dot(selected.T, weighted, precision=HIGHEST, preferred_element_type=jnp.float32)
    adjoint = jnp.zeros((NLEV, NLAT * NLON), jnp.float32)
    for member in range(FOOT):
        adjoint = adjoint.at[:, target[member]].add(foot_weight[member][None, :] * pulled)
    upward = jnp.dot(mat_vert.T, adjoint, precision=HIGHEST, preferred_element_type=jnp.float32)
    upward = upward.reshape(NLEV, NLAT, NLON)
    return chi + apply_lat(apply_lon(upward, mat_lon.T), mat_lat.T)
```

```python
import functools

import jax
import jax.numpy as jnp
from jax import lax
from jax.experimental import pallas as pl
from jax.experimental.pallas import tpu as pltpu
from jax.sharding import PartitionSpec as P

HIGHEST = lax.Precision.HIGHEST
F32 = jnp.float32
BF16 = jnp.bfloat16

LEVELS = 17
MAIN = 16
ROWS = 16
CELLS = 256
TILE = ROWS * LEVELS
OWNER = 2 * MAIN
CAP = 64
TILES = 8
VIEWERS = 8
OBS = 1024
FOOT = 4
BLOCK = 256
PARTNER = [(t, t ^ 1) for t in range(8)]
ALONG_Y = [[0, 2, 4, 6], [1, 3, 5, 7]]


def split_rows(x):
    high = x.astype(BF16)
    low = (x - high.astype(F32)).astype(BF16)
    return jnp.concatenate([high, low], axis=0)


def one_hot(index, rows):
    place = lax.broadcasted_iota(jnp.int32, (rows, index.shape[1]), 0)
    return jnp.where(place == index, 1.0, 0.0).astype(BF16)


def dot(a, b):
    return lax.dot_general(a, b, (((1,), (0,)), ((), ())), preferred_element_type=F32)


def dot_nt(a, b):
    return lax.dot_general(a, b, (((1,), (1,)), ((), ())), preferred_element_type=F32)


def pick_kernel(field_ref, serve_ref, slots_ref):
    tile = pl.program_id(0)
    for half in range(2):
        last = field_ref[0, 256 + 8 * half : 264 + 8 * half, :]
        mains = []
        lasts = []
        for quarter in range(4):
            slab = 4 * half + quarter
            index = serve_ref[0, slab : slab + 1, :]
            cell = jnp.bitwise_and(index, CELLS - 1)
            second = index >= CELLS
            rows = jnp.concatenate([field_ref[0, slab * OWNER : (slab + 1) * OWNER, :], last], axis=0)
            count = OWNER + 8
            both = dot(split_rows(rows), one_hot(cell, CELLS))
            picked = both[:count] + both[count:]
            mains.append(jnp.where(second, picked[MAIN:OWNER], picked[:MAIN]))
            at = OWNER + 2 * quarter
            lasts.append(jnp.where(second, picked[at + 1 : at + 2], picked[at : at + 1]))
        start = pl.multiple_of(tile * OWNER + half * MAIN, MAIN)
        for viewer in range(VIEWERS):
            lanes = slice(viewer * CAP, (viewer + 1) * CAP)
            slots_ref[viewer, pl.ds(start, MAIN), :] = jnp.concatenate([m[:, lanes] for m in mains], axis=1)
            slots_ref[viewer, pl.ds(256 + 2 * tile + half, 1), :] = jnp.concatenate(
                [m[:, lanes] for m in lasts], axis=1
            )


def pick(field, serve):
    return pl.pallas_call(
        pick_kernel,
        grid=(TILES,),
        in_specs=[
            pl.BlockSpec((1, TILE, CELLS), lambda j: (j, 0, 0)),
            pl.BlockSpec((1, 8, VIEWERS * CAP), lambda j: (j, 0, 0)),
        ],
        out_specs=pl.BlockSpec((VIEWERS, TILE, BLOCK), lambda j: (0, 0, 0)),
        out_shape=jax.ShapeDtypeStruct((VIEWERS, TILE, BLOCK), F32),
        compiler_params=pltpu.CompilerParams(vmem_limit_bytes=32 * 1024 * 1024),
    )(field, serve)


def mean_kernel(slots_ref, place_ref, weight_ref, mean_ref):
    values = split_rows(slots_ref[0])
    for start in range(0, OBS, BLOCK):
        lanes = slice(start, start + BLOCK)
        main = jnp.zeros((MAIN, BLOCK), F32)
        last = jnp.zeros((16, BLOCK), F32)
        for member in range(FOOT):
            place = place_ref[0, member : member + 1, lanes]
            low = jnp.bitwise_and(place, BLOCK - 1)
            high = lax.shift_right_logical(place, 8)
            weight = weight_ref[0, member : member + 1, lanes]
            both = dot(values, one_hot(low, BLOCK))
            picked = both[:TILE] + both[TILE:]
            masked = jnp.where(lax.broadcasted_iota(jnp.int32, (16, BLOCK), 0) == high, weight, 0.0)
            for part in range(16):
                main = main + picked[part * MAIN : (part + 1) * MAIN] * masked[part : part + 1]
            last = last + picked[256:TILE] * masked
        mean_ref[0, :MAIN, lanes] = main
        mean_ref[0, MAIN:, lanes] = jnp.sum(last, axis=0, keepdims=True)


def means(slots, place, weight):
    count = slots.shape[0]
    return pl.pallas_call(
        mean_kernel,
        grid=(count,),
        in_specs=[
            pl.BlockSpec((1, TILE, BLOCK), lambda v: (v, 0, 0)),
            pl.BlockSpec((1, FOOT, OBS), lambda v: (v, 0, 0)),
            pl.BlockSpec((1, FOOT, OBS), lambda v: (v, 0, 0)),
        ],
        out_specs=pl.BlockSpec((1, LEVELS, OBS), lambda v: (v, 0, 0)),
        out_shape=jax.ShapeDtypeStruct((count, LEVELS, OBS), F32),
        compiler_params=pltpu.CompilerParams(vmem_limit_bytes=32 * 1024 * 1024),
    )(slots, place, weight)


def spread_kernel(grad_ref, place_ref, weight_ref, slots_ref):
    total = jnp.zeros((2 * TILE, BLOCK), F32)
    for start in range(0, OBS, BLOCK):
        lanes = slice(start, start + BLOCK)
        grad = grad_ref[0, :, lanes]
        for member in range(FOOT):
            place = place_ref[0, member : member + 1, lanes]
            low = jnp.bitwise_and(place, BLOCK - 1)
            high = lax.shift_right_logical(place, 8)
            scaled = grad * weight_ref[0, member : member + 1, lanes]
            hit = jnp.where(lax.broadcasted_iota(jnp.int32, (16, BLOCK), 0) == high, 1.0, 0.0)
            main = scaled[:MAIN]
            main_high = main.astype(BF16)
            main_low = (main - main_high.astype(F32)).astype(BF16)
            last = scaled[MAIN:] * hit
            last_high = last.astype(BF16)
            last_low = (last - last_high.astype(F32)).astype(BF16)
            hits = [jnp.broadcast_to(hit[part : part + 1], (MAIN, BLOCK)).astype(BF16) for part in range(16)]
            rows = jnp.concatenate(
                [main_high * h for h in hits] + [last_high] + [main_low * h for h in hits] + [last_low], axis=0
            )
            total = total + dot_nt(rows, one_hot(low, BLOCK))
    slots_ref[0] = total[:TILE] + total[TILE:]


def spread(grad, place, weight):
    count = grad.shape[0]
    return pl.pallas_call(
        spread_kernel,
        grid=(count,),
        in_specs=[
            pl.BlockSpec((1, LEVELS, OBS), lambda v: (v, 0, 0)),
            pl.BlockSpec((1, FOOT, OBS), lambda v: (v, 0, 0)),
            pl.BlockSpec((1, FOOT, OBS), lambda v: (v, 0, 0)),
        ],
        out_specs=pl.BlockSpec((1, TILE, BLOCK), lambda v: (v, 0, 0)),
        out_shape=jax.ShapeDtypeStruct((count, TILE, BLOCK), F32),
        compiler_params=pltpu.CompilerParams(vmem_limit_bytes=32 * 1024 * 1024),
    )(grad, place, weight)


def put_kernel(slots_ref, serve_ref, field_ref):
    tile = pl.program_id(0)
    for half in range(2):
        start = pl.multiple_of(tile * OWNER + half * MAIN, MAIN)
        mains = [slots_ref[viewer, pl.ds(start, MAIN), :] for viewer in range(VIEWERS)]
        lasts = [slots_ref[viewer, pl.ds(256 + 2 * tile + half, 1), :] for viewer in range(VIEWERS)]
        tails = []
        for quarter in range(4):
            slab = 4 * half + quarter
            index = serve_ref[0, slab : slab + 1, :]
            cell = jnp.bitwise_and(index, CELLS - 1)
            second = index >= CELLS
            lanes = slice(quarter * CAP, (quarter + 1) * CAP)
            main = jnp.concatenate([m[:, lanes] for m in mains], axis=1)
            last = jnp.concatenate([m[:, lanes] for m in lasts], axis=1)
            row = lax.broadcasted_iota(jnp.int32, (8, VIEWERS * CAP), 0)
            tail = jnp.where(row == jnp.where(second, 1, 0), last, 0.0)
            rows = jnp.concatenate([jnp.where(second, 0.0, main), jnp.where(second, main, 0.0), tail], axis=0)
            count = OWNER + 8
            both = dot_nt(split_rows(rows), one_hot(cell, CELLS))
            back = both[:count] + both[count:]
            field_ref[0, slab * OWNER : (slab + 1) * OWNER, :] = back[:OWNER]
            tails.append(back[OWNER : OWNER + 2])
        field_ref[0, 256 + 8 * half : 264 + 8 * half, :] = jnp.concatenate(tails, axis=0)


def put(slots, serve):
    return pl.pallas_call(
        put_kernel,
        grid=(TILES,),
        in_specs=[
            pl.BlockSpec((VIEWERS, TILE, BLOCK), lambda j: (0, 0, 0)),
            pl.BlockSpec((1, 8, VIEWERS * CAP), lambda j: (j, 0, 0)),
        ],
        out_specs=pl.BlockSpec((1, TILE, CELLS), lambda j: (j, 0, 0)),
        out_shape=jax.ShapeDtypeStruct((TILES, TILE, CELLS), F32),
        compiler_params=pltpu.CompilerParams(vmem_limit_bytes=32 * 1024 * 1024),
    )(slots, serve)


def to_all_y(block):
    copies = jnp.broadcast_to(block[None], (4,) + block.shape)
    return lax.all_to_all(copies, "obs", 0, 0, axis_index_groups=ALONG_Y)


def gather_obs(block):
    other = lax.ppermute(block, "obs", PARTNER)
    return to_all_y(block), to_all_y(other)


def times_lon(near, far, lon_near, lon_far):
    def product(tiles, matrix):
        return jnp.einsum("yrc,ycd->rd", tiles, matrix, precision=HIGHEST, preferred_element_type=F32)

    return product(near, lon_near) + product(far, lon_far)


def shards(
    chi,
    mat_lon,
    mat_lat,
    mat_vert,
    chan_table,
    chan_map,
    error_weight,
    innovation,
    foot_weight,
    foot_slot,
    serve_cols,
):
    half = lax.axis_index("obs") % 2

    def near_far(x, axis):
        near = lax.dynamic_index_in_dim(x, half, axis, keepdims=False)
        far = lax.dynamic_index_in_dim(x, 1 - half, axis, keepdims=False)
        return near, far

    serve = serve_cols[0, 0].astype(F32).reshape(8, 8, CAP).transpose(1, 0, 2)
    serve = lax.all_to_all(serve, "obs", 0, 0)
    about = jnp.concatenate(
        [serve.reshape(4, OBS), foot_slot.astype(F32), foot_weight], axis=0
    )
    about = lax.all_gather(about, "lev", axis=0, tiled=False)
    serve = about[:, :4].reshape(8, 4, 2, VIEWERS * CAP).astype(jnp.int32)
    near, far = near_far(serve, 2)
    serve = jnp.concatenate([near, far], axis=1).transpose(1, 0, 2)
    slot = about[:, 4:8].astype(jnp.int32)
    weight = about[:, 8:]
    tile = (slot >> 6) & 7
    tile = (tile >> 1) + 4 * ((tile & 1) ^ half)
    slab = slot >> 9
    place = (2 * tile + (slab >> 2)) * BLOCK + (slab & 3) * CAP + (slot & (CAP - 1))

    lon_near, lon_far = near_far(mat_lon.reshape(4, 2, CELLS, CELLS), 1)

    band = lax.all_gather(chi, "lat", axis=1, tiled=True)
    field = jnp.einsum("ij,ljk->ilk", mat_lat, band, precision=HIGHEST, preferred_element_type=F32)
    field = jnp.concatenate([field[:, :MAIN].reshape(ROWS * MAIN, CELLS), field[:, MAIN]], axis=0)
    field = times_lon(*gather_obs(field), lon_near, lon_far)
    near, far = gather_obs(field)
    slots = pick(jnp.concatenate([near, far], axis=0), serve)
    mean = means(slots, place, weight)
    mean = lax.all_to_all(mean, "lev", 0, 0).reshape(8 * LEVELS, OBS)

    matches = (
        chan_map[:, None] == jnp.arange(chan_table.shape[0], dtype=jnp.int32)[None, :]
    ).astype(F32)
    selected = jnp.dot(matches, chan_table, precision=HIGHEST, preferred_element_type=F32)
    selected = jnp.dot(selected, mat_vert, precision=HIGHEST, preferred_element_type=F32)
    scaled = error_weight[:, None] * selected
    hessian = jnp.dot(selected.T, scaled, precision=HIGHEST, preferred_element_type=F32)
    constant = jnp.dot(scaled.T, innovation, precision=HIGHEST, preferred_element_type=F32)
    pulled = jnp.dot(hessian, mean, precision=HIGHEST, preferred_element_type=F32) - constant

    pulled = lax.all_to_all(pulled.reshape(8, LEVELS, OBS), "lev", 0, 0)
    slots = spread(pulled, place, weight)
    partial = put(slots, serve)
    far = jnp.sum(lax.all_to_all(partial[4:], "obs", 0, 0, axis_index_groups=ALONG_Y), axis=0)
    far = lax.ppermute(far, "obs", PARTNER)
    near = jnp.sum(lax.all_to_all(partial[:4], "obs", 0, 0, axis_index_groups=ALONG_Y), axis=0)
    field = times_lon(*gather_obs(near + far), lon_near, lon_far)
    band = lax.all_gather(field, "lat", axis=0, tiled=False)
    main = band[:, : ROWS * MAIN].reshape(8 * ROWS, MAIN, CELLS)
    last = band[:, ROWS * MAIN :].reshape(8 * ROWS, 1, CELLS)
    band = jnp.concatenate([main, last], axis=1)
    return chi + jnp.einsum("ij,jlk->lik", mat_lat, band, precision=HIGHEST, preferred_element_type=F32)


def solution(mesh):
    in_specs = (
        P("lev", "lat", "obs"),
        P(None, "obs"),
        P("lat", None),
        P(),
        P(),
        P(),
        P(),
        P(None, ("lat", "lev", "obs")),
        P(None, ("lat", "lev", "obs")),
        P(None, ("lat", "lev", "obs")),
        P("lat", ("lev", "obs"), None, None),
    )
    out_specs = P("lev", "lat", "obs")
    return jax.shard_map(shards, mesh=mesh, in_specs=in_specs, out_specs=out_specs, check_vma=False)
```

```python
import jax
import jax.numpy as jnp
from jax import lax
from jax.experimental import pallas as pl
from jax.experimental.pallas import tpu as pltpu
from jax.sharding import PartitionSpec as P

HIGHEST = lax.Precision.HIGHEST
F32 = jnp.float32
BF16 = jnp.bfloat16

LEVELS = 17
MAIN = 16
CELLS = 256
OWNER = 2 * MAIN
HALF = 4 * OWNER + 8
CAP = 64
VIEWERS = 8
OBS = 1024
FOOT = 4
BLOCK = 256
CHUNKS = 1
HALVES = 2 // CHUNKS
PARTS = 1
PART = OBS // PARTS
GROUP_MAIN = 4 * HALVES * MAIN
GROUP = GROUP_MAIN + 8
PARTNER = [(t, t ^ 1) for t in range(8)]
ALONG = [[0, 2, 4, 6], [1, 3, 5, 7]]
VMEM = 48 * 1024 * 1024


def params():
    return pltpu.CompilerParams(vmem_limit_bytes=VMEM)


def split(x):
    high = x.astype(BF16)
    return high, (x - high.astype(F32)).astype(BF16)


def split_rows(x):
    return jnp.concatenate(split(x), axis=0)


def one_hot(index, rows):
    place = lax.broadcasted_iota(jnp.int32, (rows, index.shape[1]), 0)
    return jnp.where(place == index, 1.0, 0.0).astype(BF16)


def dot(a, b):
    return lax.dot_general(a, b, (((1,), (0,)), ((), ())), preferred_element_type=F32)


def dot_nt(a, b):
    return lax.dot_general(a, b, (((1,), (1,)), ((), ())), preferred_element_type=F32)


def pick_kernel(field_ref, serve_ref, slots_ref):
    tile = pl.program_id(0)
    for half in range(HALVES):
        base = half * HALF
        last = field_ref[0, base + 4 * OWNER : base + HALF, :]
        mains = []
        lasts = []
        for quarter in range(4):
            index = serve_ref[0, 4 * half + quarter : 4 * half + quarter + 1, :]
            cell = jnp.bitwise_and(index, CELLS - 1)
            second = index >= CELLS
            start = base + quarter * OWNER
            rows = jnp.concatenate([field_ref[0, start : start + OWNER, :], last], axis=0)
            count = OWNER + 8
            both = dot(split_rows(rows), one_hot(cell, CELLS))
            picked = both[:count] + both[count:]
            mains.append(jnp.where(second, picked[MAIN:OWNER], picked[:MAIN]))
            at = OWNER + 2 * quarter
            lasts.append(jnp.where(second, picked[at + 1 : at + 2], picked[at : at + 1]))
        place = 4 * half + tile
        start = pl.multiple_of(place * MAIN, MAIN)
        for viewer in range(VIEWERS):
            lanes = slice(viewer * CAP, (viewer + 1) * CAP)
            slots_ref[viewer, pl.ds(start, MAIN), :] = jnp.concatenate([m[:, lanes] for m in mains], axis=1)
            slots_ref[viewer, pl.ds(GROUP_MAIN + place, 1), :] = jnp.concatenate([m[:, lanes] for m in lasts], axis=1)


def pick(field, serve):
    return pl.pallas_call(
        pick_kernel,
        grid=(4,),
        in_specs=[
            pl.BlockSpec((1, HALVES * HALF, CELLS), lambda y: (y, 0, 0)),
            pl.BlockSpec((1, 4 * HALVES, VIEWERS * CAP), lambda y: (y, 0, 0)),
        ],
        out_specs=pl.BlockSpec((VIEWERS, GROUP, BLOCK), lambda y: (0, 0, 0)),
        out_shape=jax.ShapeDtypeStruct((VIEWERS, GROUP, BLOCK), F32),
        compiler_params=params(),
    )(field, serve)


def mean_kernel(place_ref, weight_ref, *refs):
    slots, mean_ref = refs[:-1], refs[-1]
    mains = jnp.concatenate([s[0, :GROUP_MAIN, :] for s in slots], axis=0)
    lasts = jnp.concatenate([s[0, GROUP_MAIN : GROUP_MAIN + 4 * HALVES, :] for s in slots], axis=0)
    values = split_rows(jnp.concatenate([mains, lasts], axis=0))
    total = 16 * MAIN + 16
    for start in range(0, PART, BLOCK):
        lanes = slice(start, start + BLOCK)
        main = jnp.zeros((MAIN, BLOCK), F32)
        last = jnp.zeros((16, BLOCK), F32)
        for member in range(FOOT):
            place = place_ref[0, member : member + 1, lanes]
            low = jnp.bitwise_and(place, BLOCK - 1)
            high = lax.shift_right_logical(place, 8)
            weight = weight_ref[0, member : member + 1, lanes]
            both = dot(values, one_hot(low, BLOCK))
            picked = both[:total] + both[total:]
            masked = jnp.where(lax.broadcasted_iota(jnp.int32, (16, BLOCK), 0) == high, weight, 0.0)
            for part in range(16):
                main = main + picked[part * MAIN : (part + 1) * MAIN] * masked[part : part + 1]
            last = last + picked[16 * MAIN :] * masked
        mean_ref[0, :MAIN, lanes] = main
        mean_ref[0, MAIN:, lanes] = jnp.sum(last, axis=0, keepdims=True)


def means(slots, place, weight, part):
    return pl.pallas_call(
        mean_kernel,
        grid=(VIEWERS,),
        in_specs=[
            pl.BlockSpec((1, FOOT, PART), lambda v: (v, 0, part)),
            pl.BlockSpec((1, FOOT, PART), lambda v: (v, 0, part)),
        ]
        + [pl.BlockSpec((1, GROUP, BLOCK), lambda v: (v, 0, 0))] * len(slots),
        out_specs=pl.BlockSpec((1, LEVELS, PART), lambda v: (v, 0, 0)),
        out_shape=jax.ShapeDtypeStruct((VIEWERS, LEVELS, PART), F32),
        compiler_params=params(),
    )(place, weight, *slots)


def pull_kernel(mean_ref, hessian_ref, constant_ref, pulled_ref):
    mean = jnp.concatenate([mean_ref[m] for m in range(8)], axis=0)
    pulled = lax.dot_general(
        hessian_ref[...], mean, (((1,), (0,)), ((), ())), precision=HIGHEST, preferred_element_type=F32
    )
    pulled = pulled - constant_ref[...]
    for m in range(8):
        pulled_ref[m] = pulled[m * LEVELS : (m + 1) * LEVELS]


def pull(mean, hessian, constant, part):
    size = 8 * LEVELS
    return pl.pallas_call(
        pull_kernel,
        grid=(1,),
        in_specs=[
            pl.BlockSpec((8, LEVELS, PART), lambda i: (0, 0, 0)),
            pl.BlockSpec((size, size), lambda i: (0, 0)),
            pl.BlockSpec((size, PART), lambda i: (0, part)),
        ],
        out_specs=pl.BlockSpec((8, LEVELS, PART), lambda i: (0, 0, 0)),
        out_shape=jax.ShapeDtypeStruct((8, LEVELS, PART), F32),
        compiler_params=params(),
    )(mean, hessian, constant)


def spread_kernel(grad_ref, place_ref, weight_ref, *refs):
    groups = 2 * CHUNKS
    before, slots = refs[:-groups], refs[-groups:]
    total = jnp.zeros((2 * (16 * MAIN + 16), BLOCK), F32)
    for start in range(0, PART, BLOCK):
        lanes = slice(start, start + BLOCK)
        grad = grad_ref[0, :, lanes]
        for member in range(FOOT):
            place = place_ref[0, member : member + 1, lanes]
            low = jnp.bitwise_and(place, BLOCK - 1)
            high = lax.shift_right_logical(place, 8)
            scaled = grad * weight_ref[0, member : member + 1, lanes]
            hit = jnp.where(lax.broadcasted_iota(jnp.int32, (16, BLOCK), 0) == high, 1.0, 0.0)
            main_high, main_low = split(scaled[:MAIN])
            last_high, last_low = split(scaled[MAIN:] * hit)
            hits = [jnp.broadcast_to(hit[part : part + 1], (MAIN, BLOCK)).astype(BF16) for part in range(16)]
            rows = jnp.concatenate(
                [main_high * h for h in hits] + [last_high] + [main_low * h for h in hits] + [last_low], axis=0
            )
            total = total + dot_nt(rows, one_hot(low, BLOCK))
    total = total[: 16 * MAIN + 16] + total[16 * MAIN + 16 :]
    for group in range(groups):
        main = total[group * GROUP_MAIN : (group + 1) * GROUP_MAIN]
        at = 16 * MAIN + group * 4 * HALVES
        last = total[at : at + 4 * HALVES]
        if before:
            main = main + before[group][0, :GROUP_MAIN, :]
            last = last + before[group][0, GROUP_MAIN : GROUP_MAIN + 4 * HALVES, :]
        slots[group][0, :GROUP_MAIN, :] = main
        slots[group][0, GROUP_MAIN : GROUP_MAIN + 4 * HALVES, :] = last


def spread(grad, place, weight, before, part):
    groups = 2 * CHUNKS
    slots = pl.BlockSpec((1, GROUP, BLOCK), lambda v: (v, 0, 0))
    return pl.pallas_call(
        spread_kernel,
        grid=(VIEWERS,),
        in_specs=[
            pl.BlockSpec((1, LEVELS, PART), lambda v: (v, 0, 0)),
            pl.BlockSpec((1, FOOT, PART), lambda v: (v, 0, part)),
            pl.BlockSpec((1, FOOT, PART), lambda v: (v, 0, part)),
        ]
        + [slots] * len(before),
        out_specs=[slots] * groups,
        out_shape=[jax.ShapeDtypeStruct((VIEWERS, GROUP, BLOCK), F32)] * groups,
        compiler_params=params(),
    )(grad, place, weight, *before)


def put_kernel(slots_ref, serve_ref, field_ref):
    tile = pl.program_id(0)
    for half in range(HALVES):
        base = half * HALF
        place = 4 * half + tile
        start = pl.multiple_of(place * MAIN, MAIN)
        mains = [slots_ref[viewer, pl.ds(start, MAIN), :] for viewer in range(VIEWERS)]
        lasts = [slots_ref[viewer, pl.ds(GROUP_MAIN + place, 1), :] for viewer in range(VIEWERS)]
        tails = []
        for quarter in range(4):
            index = serve_ref[0, 4 * half + quarter : 4 * half + quarter + 1, :]
            cell = jnp.bitwise_and(index, CELLS - 1)
            second = index >= CELLS
            lanes = slice(quarter * CAP, (quarter + 1) * CAP)
            main = jnp.concatenate([m[:, lanes] for m in mains], axis=1)
            last = jnp.concatenate([m[:, lanes] for m in lasts], axis=1)
            row = lax.broadcasted_iota(jnp.int32, (8, VIEWERS * CAP), 0)
            tail = jnp.where(row == jnp.where(second, 1, 0), last, 0.0)
            rows = jnp.concatenate([jnp.where(second, 0.0, main), jnp.where(second, main, 0.0), tail], axis=0)
            count = OWNER + 8
            both = dot_nt(split_rows(rows), one_hot(cell, CELLS))
            back = both[:count] + both[count:]
            field_ref[0, base + quarter * OWNER : base + (quarter + 1) * OWNER, :] = back[:OWNER]
            tails.append(back[OWNER : OWNER + 2])
        field_ref[0, base + 4 * OWNER : base + HALF, :] = jnp.concatenate(tails, axis=0)


def put(slots, serve):
    return pl.pallas_call(
        put_kernel,
        grid=(4,),
        in_specs=[
            pl.BlockSpec((VIEWERS, GROUP, BLOCK), lambda y: (0, 0, 0)),
            pl.BlockSpec((1, 4 * HALVES, VIEWERS * CAP), lambda y: (y, 0, 0)),
        ],
        out_specs=pl.BlockSpec((1, HALVES * HALF, CELLS), lambda y: (y, 0, 0)),
        out_shape=jax.ShapeDtypeStruct((4, HALVES * HALF, CELLS), F32),
        compiler_params=params(),
    )(slots, serve)


def finish_kernel(chi_ref, lat_ref, *refs):
    bands, out_ref = refs[:-1], refs[-1]
    mains = []
    lasts = []
    for near_far in range(2):
        for half in range(2):
            ref = bands[near_far * CHUNKS + half // HALVES]
            base = (half % HALVES) * HALF
            for x in range(4):
                main = ref[x, base : base + 4 * OWNER, :].reshape(8, MAIN, CELLS)
                mains.append(jnp.swapaxes(main, 0, 1))
                lasts.append(ref[x, base + 4 * OWNER : base + HALF, :])
    for level in range(LEVELS):
        rows = jnp.concatenate([m[level] for m in mains] if level < MAIN else lasts, axis=0)
        out_ref[level] = chi_ref[level] + lax.dot_general(
            lat_ref[...], rows, (((1,), (0,)), ((), ())), precision=HIGHEST, preferred_element_type=F32
        )


def finish(chi, lat, bands):
    return pl.pallas_call(
        finish_kernel,
        out_shape=jax.ShapeDtypeStruct(chi.shape, F32),
        compiler_params=params(),
    )(chi, lat, *bands)


def to_all(block, axis):
    copies = jnp.broadcast_to(block[None], (4,) + block.shape)
    return lax.all_to_all(copies, axis, 0, 0, axis_index_groups=ALONG)


def gather_obs(block):
    other = lax.ppermute(block, "obs", PARTNER)
    return to_all(block, "obs"), to_all(other, "obs")


def times_lon(near, far, lon_near, lon_far):
    def product(tiles, matrix):
        return jnp.einsum("yrc,ycd->rd", tiles, matrix, precision=HIGHEST, preferred_element_type=F32)

    return product(near, lon_near) + product(far, lon_far)


def shards(
    chi,
    mat_lon,
    mat_lat,
    mat_vert,
    chan_table,
    chan_map,
    error_weight,
    innovation,
    foot_weight,
    foot_slot,
    serve_cols,
):
    half = lax.axis_index("obs") % 2
    core = lax.axis_index("lat") % 2

    def near_far(x, axis, which):
        near = lax.dynamic_index_in_dim(x, which, axis, keepdims=False)
        far = lax.dynamic_index_in_dim(x, 1 - which, axis, keepdims=False)
        return near, far

    feet = jnp.concatenate([foot_slot.astype(F32), foot_weight], axis=0)
    feet = lax.all_to_all(jnp.broadcast_to(feet[None], (8,) + feet.shape), "lev", 0, 0)
    serve = serve_cols[0, 0].astype(F32).reshape(8, 8, CAP).transpose(1, 0, 2)
    serve = lax.all_to_all(serve, "obs", 0, 0)
    serve = serve.reshape(8, VIEWERS * CAP)

    band_near = to_all(chi, "lat")
    band_far = lax.ppermute(band_near, "lat", PARTNER)
    lat_near, lat_far = near_far(mat_lat.reshape(16, 4, 2, 16), 2, core)
    field = jnp.einsum(
        "ixr,xlrk->ilk", lat_near, band_near, precision=HIGHEST, preferred_element_type=F32
    ) + jnp.einsum("ixr,xlrk->ilk", lat_far, band_far, precision=HIGHEST, preferred_element_type=F32)
    feet, serve, field = lax.optimization_barrier((feet, serve, field))
    chunks = []
    for chunk in range(CHUNKS):
        pieces = []
        for place in range(chunk * HALVES, (chunk + 1) * HALVES):
            rows = field[8 * place : 8 * place + 8]
            pieces += [rows[:, :MAIN].reshape(8 * MAIN, CELLS), rows[:, MAIN]]
        chunks.append(jnp.concatenate(pieces, axis=0))

    serve = lax.all_to_all(jnp.broadcast_to(serve[None], (8,) + serve.shape), "lev", 0, 0)
    serve = serve.reshape(8, 4, 2, VIEWERS * CAP).astype(jnp.int32)
    serves = [s.transpose(1, 0, 2) for s in near_far(serve, 2, half)]
    slot = feet[:, :4].astype(jnp.int32)
    weight = feet[:, 4:]
    tile = (slot >> 6) & 7
    far = (tile & 1) ^ half
    slab = slot >> 9
    if CHUNKS == 2:
        group = 2 * (slab >> 2) + far
    else:
        group = 2 * far + (slab >> 2)
    place = (4 * group + (tile >> 1)) * BLOCK + (slab & 3) * CAP + (slot & (CAP - 1))

    lons = near_far(mat_lon.reshape(4, 2, CELLS, CELLS), 1, half)
    matches = (
        chan_map[:, None] == jnp.arange(chan_table.shape[0], dtype=jnp.int32)[None, :]
    ).astype(F32)
    selected = jnp.dot(matches, chan_table, precision=HIGHEST, preferred_element_type=F32)
    selected = jnp.dot(selected, mat_vert, precision=HIGHEST, preferred_element_type=F32)
    scaled = error_weight[:, None] * selected
    hessian = jnp.dot(selected.T, scaled, precision=HIGHEST, preferred_element_type=F32)
    constant = jnp.dot(scaled.T, innovation, precision=HIGHEST, preferred_element_type=F32)

    chunks = [times_lon(*gather_obs(chunk), *lons) for chunk in chunks]
    chunks, serves, place, weight, hessian, constant = lax.optimization_barrier(
        (chunks, serves, place, weight, hessian, constant)
    )

    def serve_of(which, chunk):
        return serves[which][:, 4 * HALVES * chunk : 4 * HALVES * (chunk + 1)]

    slots = []
    for chunk in range(CHUNKS):
        for which, tiles in enumerate(gather_obs(chunks[chunk])):
            slots.append(pick(tiles, serve_of(which, chunk)))

    back = []
    for part in range(PARTS):
        mean = lax.all_to_all(means(slots, place, weight, part), "lev", 0, 0)
        back.append(lax.all_to_all(pull(mean, hessian, constant, part), "lev", 0, 0))
    slots = []
    for part in range(PARTS):
        slots = spread(back[part], place, weight, slots, part)

    bands = []
    for chunk in range(CHUNKS):
        tiles = put(slots[2 * chunk + 1], serve_of(1, chunk))
        far = jnp.sum(lax.all_to_all(tiles, "obs", 0, 0, axis_index_groups=ALONG), axis=0)
        far = lax.ppermute(far, "obs", PARTNER)
        tiles = put(slots[2 * chunk], serve_of(0, chunk))
        near = jnp.sum(lax.all_to_all(tiles, "obs", 0, 0, axis_index_groups=ALONG), axis=0)
        field = times_lon(*gather_obs(near + far), *lons)
        band_near = to_all(field, "lat")
        bands.append((band_near, lax.ppermute(band_near, "lat", PARTNER)))
    lat = jnp.stack(
        [m.reshape(16, 4, 2, 8).transpose(0, 2, 1, 3) for m in (lat_near, lat_far)], axis=1
    ).reshape(16, 128)
    return finish(chi, lat, [b[0] for b in bands] + [b[1] for b in bands])


def solution(mesh):
    in_specs = (
        P("lev", "lat", "obs"),
        P(None, "obs"),
        P("lat", None),
        P(),
        P(),
        P(),
        P(),
        P(None, ("lat", "lev", "obs")),
        P(None, ("lat", "lev", "obs")),
        P(None, ("lat", "lev", "obs")),
        P("lat", ("lev", "obs"), None, None),
    )
    out_specs = P("lev", "lat", "obs")
    return jax.shard_map(shards, mesh=mesh, in_specs=in_specs, out_specs=out_specs, check_vma=False)
```

```python
import jax
import jax.numpy as jnp
from jax import lax
from jax.experimental import pallas as pl
from jax.experimental.pallas import tpu as pltpu
from jax.sharding import PartitionSpec as P

HIGHEST = lax.Precision.HIGHEST
F32 = jnp.float32
BF16 = jnp.bfloat16

LEVELS = 17
MAIN = 16
CELLS = 256
OWNER = 2 * MAIN
HALF = 4 * OWNER + 8
CAP = 64
VIEWERS = 8
OBS = 1024
FOOT = 4
BLOCK = 256
HALVES = 2
GROUP_MAIN = 4 * HALVES * MAIN
GROUP = GROUP_MAIN + 8
PARTNER = [(t, t ^ 1) for t in range(8)]
ALONG = [[0, 2, 4, 6], [1, 3, 5, 7]]
VMEM = 48 * 1024 * 1024


def params():
    return pltpu.CompilerParams(vmem_limit_bytes=VMEM)


def split(x):
    high = x.astype(BF16)
    return high, (x - high.astype(F32)).astype(BF16)


def split_rows(x):
    return jnp.concatenate(split(x), axis=0)


def one_hot(index, rows):
    place = lax.broadcasted_iota(jnp.int32, (rows, index.shape[1]), 0)
    return jnp.where(place == index, 1.0, 0.0).astype(BF16)


def dot(a, b):
    return lax.dot_general(a, b, (((1,), (0,)), ((), ())), preferred_element_type=F32)


def dot_nt(a, b):
    return lax.dot_general(a, b, (((1,), (1,)), ((), ())), preferred_element_type=F32)


def pick_kernel(field_ref, serve_ref, slots_ref):
    tile = pl.program_id(0)
    for half in range(HALVES):
        base = half * HALF
        last = field_ref[0, base + 4 * OWNER : base + HALF, :]
        mains = []
        lasts = []
        for quarter in range(4):
            index = serve_ref[0, 4 * half + quarter : 4 * half + quarter + 1, :]
            cell = jnp.bitwise_and(index, CELLS - 1)
            second = index >= CELLS
            start = base + quarter * OWNER
            rows = jnp.concatenate([field_ref[0, start : start + OWNER, :], last], axis=0)
            count = OWNER + 8
            both = dot(split_rows(rows), one_hot(cell, CELLS))
            picked = both[:count] + both[count:]
            mains.append(jnp.where(second, picked[MAIN:OWNER], picked[:MAIN]))
            at = OWNER + 2 * quarter
            lasts.append(jnp.where(second, picked[at + 1 : at + 2], picked[at : at + 1]))
        place = 4 * half + tile
        start = pl.multiple_of(place * MAIN, MAIN)
        for viewer in range(VIEWERS):
            lanes = slice(viewer * CAP, (viewer + 1) * CAP)
            slots_ref[viewer, pl.ds(start, MAIN), :] = jnp.concatenate([m[:, lanes] for m in mains], axis=1)
            slots_ref[viewer, pl.ds(GROUP_MAIN + place, 1), :] = jnp.concatenate([m[:, lanes] for m in lasts], axis=1)


def pick(field, serve):
    return pl.pallas_call(
        pick_kernel,
        grid=(4,),
        in_specs=[
            pl.BlockSpec((1, HALVES * HALF, CELLS), lambda y: (y, 0, 0)),
            pl.BlockSpec((1, 4 * HALVES, VIEWERS * CAP), lambda y: (y, 0, 0)),
        ],
        out_specs=pl.BlockSpec((VIEWERS, GROUP, BLOCK), lambda y: (0, 0, 0)),
        out_shape=jax.ShapeDtypeStruct((VIEWERS, GROUP, BLOCK), F32),
        compiler_params=params(),
    )(field, serve)


def mean_kernel(place_ref, weight_ref, *refs):
    slots, mean_ref = refs[:-1], refs[-1]
    mains = jnp.concatenate([s[0, :GROUP_MAIN, :] for s in slots], axis=0)
    lasts = jnp.concatenate([s[0, GROUP_MAIN : GROUP_MAIN + 4 * HALVES, :] for s in slots], axis=0)
    values = split_rows(jnp.concatenate([mains, lasts], axis=0))
    total = 16 * MAIN + 16
    for start in range(0, OBS, BLOCK):
        lanes = slice(start, start + BLOCK)
        main = jnp.zeros((MAIN, BLOCK), F32)
        last = jnp.zeros((16, BLOCK), F32)
        for member in range(FOOT):
            place = place_ref[0, member : member + 1, lanes]
            low = jnp.bitwise_and(place, BLOCK - 1)
            high = lax.shift_right_logical(place, 8)
            weight = weight_ref[0, member : member + 1, lanes]
            both = dot(values, one_hot(low, BLOCK))
            picked = both[:total] + both[total:]
            masked = jnp.where(lax.broadcasted_iota(jnp.int32, (16, BLOCK), 0) == high, weight, 0.0)
            for part in range(16):
                main = main + picked[part * MAIN : (part + 1) * MAIN] * masked[part : part + 1]
            last = last + picked[16 * MAIN :] * masked
        mean_ref[0, :MAIN, lanes] = main
        mean_ref[0, MAIN:, lanes] = jnp.sum(last, axis=0, keepdims=True)


def means(slots, place, weight):
    return pl.pallas_call(
        mean_kernel,
        grid=(VIEWERS,),
        in_specs=[
            pl.BlockSpec((1, FOOT, OBS), lambda v: (v, 0, 0)),
            pl.BlockSpec((1, FOOT, OBS), lambda v: (v, 0, 0)),
        ]
        + [pl.BlockSpec((1, GROUP, BLOCK), lambda v: (v, 0, 0))] * len(slots),
        out_specs=pl.BlockSpec((1, LEVELS, OBS), lambda v: (v, 0, 0)),
        out_shape=jax.ShapeDtypeStruct((VIEWERS, LEVELS, OBS), F32),
        compiler_params=params(),
    )(place, weight, *slots)


def pull_kernel(mean_ref, hessian_ref, constant_ref, pulled_ref):
    mean = jnp.concatenate([mean_ref[m] for m in range(8)], axis=0)
    pulled = lax.dot_general(
        hessian_ref[...], mean, (((1,), (0,)), ((), ())), precision=HIGHEST, preferred_element_type=F32
    )
    pulled = pulled - constant_ref[...]
    for m in range(8):
        pulled_ref[m] = pulled[m * LEVELS : (m + 1) * LEVELS]


def pull(mean, hessian, constant):
    size = 8 * LEVELS
    return pl.pallas_call(
        pull_kernel,
        grid=(1,),
        in_specs=[
            pl.BlockSpec((8, LEVELS, OBS), lambda i: (0, 0, 0)),
            pl.BlockSpec((size, size), lambda i: (0, 0)),
            pl.BlockSpec((size, OBS), lambda i: (0, 0)),
        ],
        out_specs=pl.BlockSpec((8, LEVELS, OBS), lambda i: (0, 0, 0)),
        out_shape=jax.ShapeDtypeStruct((8, LEVELS, OBS), F32),
        compiler_params=params(),
    )(mean, hessian, constant)


def spread_kernel(grad_ref, place_ref, weight_ref, *refs):
    slots = refs
    total = jnp.zeros((2 * (16 * MAIN + 16), BLOCK), F32)
    for start in range(0, OBS, BLOCK):
        lanes = slice(start, start + BLOCK)
        grad = grad_ref[0, :, lanes]
        for member in range(FOOT):
            place = place_ref[0, member : member + 1, lanes]
            low = jnp.bitwise_and(place, BLOCK - 1)
            high = lax.shift_right_logical(place, 8)
            scaled = grad * weight_ref[0, member : member + 1, lanes]
            hit = jnp.where(lax.broadcasted_iota(jnp.int32, (16, BLOCK), 0) == high, 1.0, 0.0)
            main_high, main_low = split(scaled[:MAIN])
            last_high, last_low = split(scaled[MAIN:] * hit)
            hits = [jnp.broadcast_to(hit[part : part + 1], (MAIN, BLOCK)).astype(BF16) for part in range(16)]
            rows = jnp.concatenate(
                [main_high * h for h in hits] + [last_high] + [main_low * h for h in hits] + [last_low], axis=0
            )
            total = total + dot_nt(rows, one_hot(low, BLOCK))
    total = total[: 16 * MAIN + 16] + total[16 * MAIN + 16 :]
    for group in range(2):
        main = total[group * GROUP_MAIN : (group + 1) * GROUP_MAIN]
        at = 16 * MAIN + group * 4 * HALVES
        last = total[at : at + 4 * HALVES]
        slots[group][0, :GROUP_MAIN, :] = main
        slots[group][0, GROUP_MAIN : GROUP_MAIN + 4 * HALVES, :] = last


def spread(grad, place, weight):
    slots = pl.BlockSpec((1, GROUP, BLOCK), lambda v: (v, 0, 0))
    return pl.pallas_call(
        spread_kernel,
        grid=(VIEWERS,),
        in_specs=[
            pl.BlockSpec((1, LEVELS, OBS), lambda v: (v, 0, 0)),
            pl.BlockSpec((1, FOOT, OBS), lambda v: (v, 0, 0)),
            pl.BlockSpec((1, FOOT, OBS), lambda v: (v, 0, 0)),
        ],
        out_specs=[slots] * 2,
        out_shape=[jax.ShapeDtypeStruct((VIEWERS, GROUP, BLOCK), F32)] * 2,
        compiler_params=params(),
    )(grad, place, weight)


def put_kernel(slots_ref, serve_ref, field_ref):
    tile = pl.program_id(0)
    for half in range(HALVES):
        base = half * HALF
        place = 4 * half + tile
        start = pl.multiple_of(place * MAIN, MAIN)
        mains = [slots_ref[viewer, pl.ds(start, MAIN), :] for viewer in range(VIEWERS)]
        lasts = [slots_ref[viewer, pl.ds(GROUP_MAIN + place, 1), :] for viewer in range(VIEWERS)]
        tails = []
        for quarter in range(4):
            index = serve_ref[0, 4 * half + quarter : 4 * half + quarter + 1, :]
            cell = jnp.bitwise_and(index, CELLS - 1)
            second = index >= CELLS
            lanes = slice(quarter * CAP, (quarter + 1) * CAP)
            main = jnp.concatenate([m[:, lanes] for m in mains], axis=1)
            last = jnp.concatenate([m[:, lanes] for m in lasts], axis=1)
            row = lax.broadcasted_iota(jnp.int32, (8, VIEWERS * CAP), 0)
            tail = jnp.where(row == jnp.where(second, 1, 0), last, 0.0)
            rows = jnp.concatenate([jnp.where(second, 0.0, main), jnp.where(second, main, 0.0), tail], axis=0)
            count = OWNER + 8
            both = dot_nt(split_rows(rows), one_hot(cell, CELLS))
            back = both[:count] + both[count:]
            field_ref[0, base + quarter * OWNER : base + (quarter + 1) * OWNER, :] = back[:OWNER]
            tails.append(back[OWNER : OWNER + 2])
        field_ref[0, base + 4 * OWNER : base + HALF, :] = jnp.concatenate(tails, axis=0)


def put(slots, serve):
    return pl.pallas_call(
        put_kernel,
        grid=(4,),
        in_specs=[
            pl.BlockSpec((VIEWERS, GROUP, BLOCK), lambda y: (0, 0, 0)),
            pl.BlockSpec((1, 4 * HALVES, VIEWERS * CAP), lambda y: (y, 0, 0)),
        ],
        out_specs=pl.BlockSpec((1, HALVES * HALF, CELLS), lambda y: (y, 0, 0)),
        out_shape=jax.ShapeDtypeStruct((4, HALVES * HALF, CELLS), F32),
        compiler_params=params(),
    )(slots, serve)


def finish_kernel(chi_ref, lat_ref, *refs):
    bands, out_ref = refs[:-1], refs[-1]
    mains = []
    lasts = []
    for near_far in range(2):
        for half in range(2):
            ref = bands[near_far]
            base = half * HALF
            for x in range(4):
                main = ref[x, base : base + 4 * OWNER, :].reshape(8, MAIN, CELLS)
                mains.append(jnp.swapaxes(main, 0, 1))
                lasts.append(ref[x, base + 4 * OWNER : base + HALF, :])
    for level in range(LEVELS):
        rows = jnp.concatenate([m[level] for m in mains] if level < MAIN else lasts, axis=0)
        out_ref[level] = chi_ref[level] + lax.dot_general(
            lat_ref[...], rows, (((1,), (0,)), ((), ())), precision=HIGHEST, preferred_element_type=F32
        )


def finish(chi, lat, bands):
    return pl.pallas_call(
        finish_kernel,
        out_shape=jax.ShapeDtypeStruct(chi.shape, F32),
        compiler_params=params(),
    )(chi, lat, *bands)


def to_all(block, axis):
    copies = jnp.broadcast_to(block[None], (4,) + block.shape)
    return lax.all_to_all(copies, axis, 0, 0, axis_index_groups=ALONG)


def to_sum(tiles):
    return jnp.sum(lax.all_to_all(tiles, "obs", 0, 0, axis_index_groups=ALONG), axis=0)


def product(tiles, matrix):
    return jnp.einsum("yrc,ycd->rd", tiles, matrix, precision=HIGHEST, preferred_element_type=F32)


def shards(
    chi,
    mat_lon,
    mat_lat,
    mat_vert,
    chan_table,
    chan_map,
    error_weight,
    innovation,
    foot_weight,
    foot_slot,
    serve_cols,
):
    half = lax.axis_index("obs") % 2
    core = lax.axis_index("lat") % 2

    def near_far(x, axis, which):
        near = lax.dynamic_index_in_dim(x, which, axis, keepdims=False)
        far = lax.dynamic_index_in_dim(x, 1 - which, axis, keepdims=False)
        return near, far

    tile = (foot_slot >> 6) & 7
    slab = foot_slot >> 9
    group = 2 * ((tile & 1) ^ half) + (slab >> 2)
    place = (4 * group + (tile >> 1)) * BLOCK + (slab & 3) * CAP + (foot_slot & (CAP - 1))

    serve = serve_cols[0, 0].astype(F32).reshape(8, 4, 2, CAP).transpose(2, 1, 0, 3)
    near, far = near_far(serve, 0, half)
    piece = lax.dynamic_index_in_dim(
        mat_lon.reshape(8, CELLS, CELLS), lax.axis_index("lat"), 0, keepdims=False
    )
    piece = jnp.concatenate([piece, far.reshape(8, CELLS)], axis=0)
    piece = lax.ppermute(piece, "obs", PARTNER)
    other_lon = lax.all_gather(piece[:CELLS], "lat", axis=0, tiled=False)
    lon_near, lon_far = near_far(mat_lon.reshape(4, 2, CELLS, CELLS), 1, half)
    other_near, other_far = near_far(other_lon.reshape(4, 2, CELLS, CELLS), 1, half)

    band_near = to_all(chi, "lat")
    band_far = lax.ppermute(band_near, "lat", PARTNER)
    lat_near, lat_far = near_far(mat_lat.reshape(16, 4, 2, 16), 2, core)
    field = jnp.einsum(
        "ixr,xlrk->ilk", lat_near, band_near, precision=HIGHEST, preferred_element_type=F32
    ) + jnp.einsum("ixr,xlrk->ilk", lat_far, band_far, precision=HIGHEST, preferred_element_type=F32)
    pieces = []
    for part in range(HALVES):
        rows = field[8 * part : 8 * part + 8]
        pieces += [rows[:, :MAIN].reshape(8 * MAIN, CELLS), rows[:, MAIN]]
    field = jnp.concatenate(pieces, axis=0)

    matches = (
        chan_map[:, None] == jnp.arange(chan_table.shape[0], dtype=jnp.int32)[None, :]
    ).astype(F32)
    selected = jnp.dot(matches, chan_table, precision=HIGHEST, preferred_element_type=F32)
    selected = jnp.dot(selected, mat_vert, precision=HIGHEST, preferred_element_type=F32)
    scaled = error_weight[:, None] * selected
    hessian = jnp.dot(selected.T, scaled, precision=HIGHEST, preferred_element_type=F32)
    constant = jnp.dot(scaled.T, innovation, precision=HIGHEST, preferred_element_type=F32)
    lat = jnp.stack(
        [m.reshape(16, 4, 2, 8).transpose(0, 2, 1, 3) for m in (lat_near, lat_far)], axis=1
    ).reshape(16, 128)

    other = lax.ppermute(field, "obs", PARTNER)
    near_tiles = to_all(field, "obs")
    serve = jnp.stack([near, piece[CELLS:].reshape(4, VIEWERS, CAP)], axis=1)
    serve = lax.all_to_all(serve, "obs", 0, 0, axis_index_groups=ALONG)
    far_tiles = to_all(other, "obs")
    tile_near = product(near_tiles, lon_near) + product(far_tiles, lon_far)
    tile_far = product(near_tiles, other_near) + product(far_tiles, other_far)

    about = jnp.concatenate([serve.reshape(4, OBS), place.astype(F32), foot_weight], axis=0)
    about, tile_near, tile_far, hessian, constant, lat = lax.optimization_barrier(
        (about, tile_near, tile_far, hessian, constant, lat)
    )
    about = about[None]
    for step in (4, 2, 1):
        other = lax.ppermute(about, "lev", [(m, m ^ step) for m in range(8)])
        upper = (lax.axis_index("lev") // step) % 2
        pair = jnp.where(upper == 0, jnp.stack([about, other], 1), jnp.stack([other, about], 1))
        about = pair.reshape((-1,) + about.shape[1:])
    weight = about[:, 8:]
    place = about[:, 4:8].astype(jnp.int32)
    serve = about[:, :4].reshape(8, 4, 2, VIEWERS * CAP).astype(jnp.int32).transpose(2, 1, 0, 3)
    near = pick(to_all(tile_near, "obs"), serve[0])
    far = pick(to_all(tile_far, "obs"), serve[1])

    mean = lax.all_to_all(means([near, far], place, weight), "lev", 0, 0)
    pulled = lax.all_to_all(pull(mean, hessian, constant), "lev", 0, 0)
    near, far = spread(pulled, place, weight)

    far = to_sum(put(far, serve[1]))
    near = to_sum(put(near, serve[0]))
    far_tiles = to_all(far, "obs")
    near_tiles = to_all(near, "obs")
    far = product(far_tiles, other_far) + product(near_tiles, other_near)
    far = lax.ppermute(far, "obs", PARTNER)
    field = product(far_tiles, lon_far) + product(near_tiles, lon_near) + far
    band_near = to_all(field, "lat")
    band_far = lax.ppermute(band_near, "lat", PARTNER)
    return finish(chi, lat, [band_near, band_far])


def solution(mesh):
    in_specs = (
        P("lev", "lat", "obs"),
        P(None, "obs"),
        P("lat", None),
        P(),
        P(),
        P(),
        P(),
        P(None, ("lat", "lev", "obs")),
        P(None, ("lat", "lev", "obs")),
        P(None, ("lat", "lev", "obs")),
        P("lat", ("lev", "obs"), None, None),
    )
    out_specs = P("lev", "lat", "obs")
    return jax.shard_map(shards, mesh=mesh, in_specs=in_specs, out_specs=out_specs, check_vma=False)
```

```python
import functools

import jax
import jax.numpy as jnp
from jax import lax
from jax.experimental import pallas as pl
from jax.experimental.pallas import tpu as pltpu
from jax.sharding import PartitionSpec as P

HIGHEST = lax.Precision.HIGHEST
F32 = jnp.float32
BF16 = jnp.bfloat16

LEVELS = 17
MAIN = 16
CELLS = 256
OWNER = 2 * MAIN
HALF = 4 * OWNER + 8
CAP = 64
VIEWERS = 8
OBS = 1024
FOOT = 4
BLOCK = 256
HALVES = 2
GROUP_MAIN = 4 * HALVES * MAIN
GROUP = GROUP_MAIN + 8
LANES = 128
LISTS = 32
COLUMN = MAIN * 8 + 8
PARTNER = [(t, t ^ 1) for t in range(8)]
ALONG = [[0, 2, 4, 6], [1, 3, 5, 7]]
VMEM = 48 * 1024 * 1024


def params():
    return pltpu.CompilerParams(vmem_limit_bytes=VMEM)


def split(x):
    high = x.astype(BF16)
    return high, (x - high.astype(F32)).astype(BF16)


def split_rows(x):
    return jnp.concatenate(split(x), axis=0)


def one_hot(index, rows):
    place = lax.broadcasted_iota(jnp.int32, (rows, index.shape[1]), 0)
    return jnp.where(place == index, 1.0, 0.0).astype(BF16)


def dot(a, b):
    return lax.dot_general(a, b, (((1,), (0,)), ((), ())), preferred_element_type=F32)


def dot_nt(a, b):
    return lax.dot_general(a, b, (((1,), (1,)), ((), ())), preferred_element_type=F32)


def lists_of(about_ref, tile, which):
    lists = []
    for slab in range(8):
        rows = about_ref[slab, pl.ds(pl.multiple_of(8 * tile, 8), 8), :]
        rows = [rows[4 * which + i : 4 * which + i + 1] for i in range(4)]
        lists.append(jnp.concatenate(rows, axis=1).astype(jnp.int32))
    return lists


def feet_of(about_ref, member, start):
    def row(first):
        at = first + 8 * member + start // LANES
        return jnp.concatenate([about_ref[0, at : at + 1, :], about_ref[0, at + 1 : at + 2, :]], axis=1)

    place = row(LISTS).astype(jnp.int32)
    return jnp.bitwise_and(place, BLOCK - 1), lax.shift_right_logical(place, 8), row(2 * LISTS)


def pick_kernel(which, field_ref, about_ref, slots_ref):
    tile = pl.program_id(0)
    lists = lists_of(about_ref, tile, which)
    for half in range(HALVES):
        base = half * HALF
        last = field_ref[0, base + 4 * OWNER : base + HALF, :]
        mains = []
        lasts = []
        for quarter in range(4):
            index = lists[4 * half + quarter]
            cell = jnp.bitwise_and(index, CELLS - 1)
            second = index >= CELLS
            start = base + quarter * OWNER
            rows = jnp.concatenate([field_ref[0, start : start + OWNER, :], last], axis=0)
            count = OWNER + 8
            both = dot(split_rows(rows), one_hot(cell, CELLS))
            picked = both[:count] + both[count:]
            mains.append(jnp.where(second, picked[MAIN:OWNER], picked[:MAIN]))
            at = OWNER + 2 * quarter
            lasts.append(jnp.where(second, picked[at + 1 : at + 2], picked[at : at + 1]))
        place = 4 * half + tile
        start = pl.multiple_of(place * MAIN, MAIN)
        for viewer in range(VIEWERS):
            lanes = slice(viewer * CAP, (viewer + 1) * CAP)
            slots_ref[viewer, pl.ds(start, MAIN), :] = jnp.concatenate([m[:, lanes] for m in mains], axis=1)
            slots_ref[viewer, pl.ds(GROUP_MAIN + place, 1), :] = jnp.concatenate([m[:, lanes] for m in lasts], axis=1)


ABOUT = (8, 3 * LISTS, LANES)


def pick(field, about, which):
    return pl.pallas_call(
        functools.partial(pick_kernel, which),
        grid=(4,),
        in_specs=[
            pl.BlockSpec((1, HALVES * HALF, CELLS), lambda y: (y, 0, 0)),
            pl.BlockSpec(ABOUT, lambda y: (0, 0, 0)),
        ],
        out_specs=pl.BlockSpec((VIEWERS, GROUP, BLOCK), lambda y: (0, 0, 0)),
        out_shape=jax.ShapeDtypeStruct((VIEWERS, GROUP, BLOCK), F32),
        compiler_params=params(),
    )(field, about)


def mean_kernel(about_ref, near_ref, far_ref, mean_ref):
    slots = near_ref, far_ref
    mains = jnp.concatenate([s[0, :GROUP_MAIN, :] for s in slots], axis=0)
    lasts = jnp.concatenate([s[0, GROUP_MAIN : GROUP_MAIN + 4 * HALVES, :] for s in slots], axis=0)
    values = split_rows(jnp.concatenate([mains, lasts], axis=0))
    total = 16 * MAIN + 16
    for start in range(0, OBS, BLOCK):
        main = jnp.zeros((MAIN, BLOCK), F32)
        last = jnp.zeros((16, BLOCK), F32)
        for member in range(FOOT):
            low, high, weight = feet_of(about_ref, member, start)
            both = dot(values, one_hot(low, BLOCK))
            picked = both[:total] + both[total:]
            masked = jnp.where(lax.broadcasted_iota(jnp.int32, (16, BLOCK), 0) == high, weight, 0.0)
            for part in range(16):
                main = main + picked[part * MAIN : (part + 1) * MAIN] * masked[part : part + 1]
            last = last + picked[16 * MAIN :] * masked
        last = jnp.sum(last, axis=0, keepdims=True)
        for piece in range(BLOCK // LANES):
            lanes = slice(piece * LANES, (piece + 1) * LANES)
            at = start // LANES + piece
            mean_ref[0, at * MAIN : (at + 1) * MAIN, :] = main[:, lanes]
            mean_ref[0, 8 * MAIN + at : 8 * MAIN + at + 1, :] = last[:, lanes]


def means(near, far, about):
    slots = pl.BlockSpec((1, GROUP, BLOCK), lambda v: (v, 0, 0))
    return pl.pallas_call(
        mean_kernel,
        grid=(VIEWERS,),
        in_specs=[pl.BlockSpec((1,) + ABOUT[1:], lambda v: (v, 0, 0)), slots, slots],
        out_specs=pl.BlockSpec((1, COLUMN, LANES), lambda v: (v, 0, 0)),
        out_shape=jax.ShapeDtypeStruct((VIEWERS, COLUMN, LANES), F32),
        compiler_params=params(),
    )(about, near, far)


def pull_kernel(mean_ref, hessian_ref, constant_ref, pulled_ref):
    columns = []
    for at in range(8):
        pieces = [mean_ref[m, at * MAIN : (at + 1) * MAIN, :] for m in range(8)]
        pieces += [mean_ref[m, 8 * MAIN + at : 8 * MAIN + at + 1, :] for m in range(8)]
        columns.append(jnp.concatenate(pieces, axis=0))
    pulled = lax.dot_general(
        hessian_ref[...],
        jnp.concatenate(columns, axis=1),
        (((1,), (0,)), ((), ())),
        precision=HIGHEST,
        preferred_element_type=F32,
    )
    pulled = pulled - constant_ref[...]
    for at in range(8):
        lanes = slice(at * LANES, (at + 1) * LANES)
        for m in range(8):
            pulled_ref[m, at * MAIN : (at + 1) * MAIN, :] = pulled[m * MAIN : (m + 1) * MAIN, lanes]
            pulled_ref[m, 8 * MAIN + at : 8 * MAIN + at + 1, :] = pulled[8 * MAIN + m : 8 * MAIN + m + 1, lanes]


def pull(mean, hessian, constant):
    return pl.pallas_call(
        pull_kernel,
        out_shape=jax.ShapeDtypeStruct((8, COLUMN, LANES), F32),
        compiler_params=params(),
    )(mean, hessian, constant)


def spread_kernel(grad_ref, about_ref, near_ref, far_ref):
    count = 16 * MAIN + 16
    total = jnp.zeros((2 * count, BLOCK), F32)
    for start in range(0, OBS, BLOCK):
        main = []
        last = []
        for at in range(start // LANES, (start + BLOCK) // LANES):
            main.append(grad_ref[0, at * MAIN : (at + 1) * MAIN, :])
            last.append(grad_ref[0, 8 * MAIN + at : 8 * MAIN + at + 1, :])
        main = jnp.concatenate(main, axis=1)
        last = jnp.concatenate(last, axis=1)
        for member in range(FOOT):
            low, high, weight = feet_of(about_ref, member, start)
            hit = jnp.where(lax.broadcasted_iota(jnp.int32, (16, BLOCK), 0) == high, 1.0, 0.0)
            main_high, main_low = split(main * weight)
            last_high, last_low = split(last * weight * hit)
            hits = [jnp.broadcast_to(hit[part : part + 1], (MAIN, BLOCK)).astype(BF16) for part in range(16)]
            rows = jnp.concatenate(
                [main_high * h for h in hits] + [last_high] + [main_low * h for h in hits] + [last_low], axis=0
            )
            total = total + dot_nt(rows, one_hot(low, BLOCK))
    total = total[:count] + total[count:]
    for group, slots_ref in enumerate((near_ref, far_ref)):
        slots_ref[0, :GROUP_MAIN, :] = total[group * GROUP_MAIN : (group + 1) * GROUP_MAIN]
        at = 16 * MAIN + group * 4 * HALVES
        slots_ref[0, GROUP_MAIN : GROUP_MAIN + 4 * HALVES, :] = total[at : at + 4 * HALVES]


def spread(grad, about):
    slots = pl.BlockSpec((1, GROUP, BLOCK), lambda v: (v, 0, 0))
    return pl.pallas_call(
        spread_kernel,
        grid=(VIEWERS,),
        in_specs=[
            pl.BlockSpec((1, COLUMN, LANES), lambda v: (v, 0, 0)),
            pl.BlockSpec((1,) + ABOUT[1:], lambda v: (v, 0, 0)),
        ],
        out_specs=[slots] * 2,
        out_shape=[jax.ShapeDtypeStruct((VIEWERS, GROUP, BLOCK), F32)] * 2,
        compiler_params=params(),
    )(grad, about)


def put_kernel(which, slots_ref, about_ref, field_ref):
    tile = pl.program_id(0)
    lists = lists_of(about_ref, tile, which)
    for half in range(HALVES):
        base = half * HALF
        place = 4 * half + tile
        start = pl.multiple_of(place * MAIN, MAIN)
        mains = [slots_ref[viewer, pl.ds(start, MAIN), :] for viewer in range(VIEWERS)]
        lasts = [slots_ref[viewer, pl.ds(GROUP_MAIN + place, 1), :] for viewer in range(VIEWERS)]
        tails = []
        for quarter in range(4):
            index = lists[4 * half + quarter]
            cell = jnp.bitwise_and(index, CELLS - 1)
            second = index >= CELLS
            lanes = slice(quarter * CAP, (quarter + 1) * CAP)
            main = jnp.concatenate([m[:, lanes] for m in mains], axis=1)
            last = jnp.concatenate([m[:, lanes] for m in lasts], axis=1)
            row = lax.broadcasted_iota(jnp.int32, (8, VIEWERS * CAP), 0)
            tail = jnp.where(row == jnp.where(second, 1, 0), last, 0.0)
            rows = jnp.concatenate([jnp.where(second, 0.0, main), jnp.where(second, main, 0.0), tail], axis=0)
            count = OWNER + 8
            both = dot_nt(split_rows(rows), one_hot(cell, CELLS))
            back = both[:count] + both[count:]
            field_ref[0, base + quarter * OWNER : base + (quarter + 1) * OWNER, :] = back[:OWNER]
            tails.append(back[OWNER : OWNER + 2])
        field_ref[0, base + 4 * OWNER : base + HALF, :] = jnp.concatenate(tails, axis=0)


def put(slots, about, which):
    return pl.pallas_call(
        functools.partial(put_kernel, which),
        grid=(4,),
        in_specs=[
            pl.BlockSpec((VIEWERS, GROUP, BLOCK), lambda y: (0, 0, 0)),
            pl.BlockSpec(ABOUT, lambda y: (0, 0, 0)),
        ],
        out_specs=pl.BlockSpec((1, HALVES * HALF, CELLS), lambda y: (y, 0, 0)),
        out_shape=jax.ShapeDtypeStruct((4, HALVES * HALF, CELLS), F32),
        compiler_params=params(),
    )(slots, about)


def add_kernel(parts_ref, sums_ref):
    total = parts_ref[0] + parts_ref[1] + parts_ref[2] + parts_ref[3]
    for copy in range(4):
        sums_ref[copy] = total


def add(parts):
    return pl.pallas_call(
        add_kernel, out_shape=jax.ShapeDtypeStruct(parts.shape, F32), compiler_params=params()
    )(parts)


def start_kernel(lat_ref, near_ref, far_ref, serve_ref, field_ref, copies_ref):
    size = HALVES * HALF
    copies_ref[:, size:, :LANES] = serve_ref[...]
    copies_ref[:, size:, LANES:] = jnp.zeros_like(serve_ref)
    levels = []
    for level in range(LEVELS):
        rows = jnp.concatenate([ref[x, level] for ref in (near_ref, far_ref) for x in range(4)], axis=0)
        levels.append(
            lax.dot_general(
                lat_ref[...], rows, (((1,), (0,)), ((), ())), precision=HIGHEST, preferred_element_type=F32
            )
        )
    main = jnp.swapaxes(jnp.stack(levels[:MAIN], axis=0), 0, 1)
    main = main.reshape(16 * MAIN, CELLS)
    for half in range(HALVES):
        rows = main[half * 8 * MAIN : (half + 1) * 8 * MAIN]
        last = levels[MAIN][8 * half : 8 * half + 8]
        base = half * HALF
        field_ref[base : base + 8 * MAIN, :] = rows
        field_ref[base + 8 * MAIN : base + HALF, :] = last
        for copy in range(4):
            copies_ref[copy, base : base + 8 * MAIN, :] = rows
            copies_ref[copy, base + 8 * MAIN : base + HALF, :] = last


def start(lat, near, far, serve):
    size = HALVES * HALF
    return pl.pallas_call(
        start_kernel,
        out_shape=[
            jax.ShapeDtypeStruct((size, CELLS), F32),
            jax.ShapeDtypeStruct((4, size + 8, CELLS), F32),
        ],
        compiler_params=params(),
    )(lat, near, far, serve)


def finish_kernel(chi_ref, lat_ref, *refs):
    bands, out_ref = refs[:-1], refs[-1]
    mains = []
    lasts = []
    for near_far in range(2):
        for half in range(2):
            ref = bands[near_far]
            base = half * HALF
            for x in range(4):
                main = ref[x, base : base + 4 * OWNER, :].reshape(8, MAIN, CELLS)
                mains.append(jnp.swapaxes(main, 0, 1))
                lasts.append(ref[x, base + 4 * OWNER : base + HALF, :])
    for level in range(LEVELS):
        rows = jnp.concatenate([m[level] for m in mains] if level < MAIN else lasts, axis=0)
        out_ref[level] = chi_ref[level] + lax.dot_general(
            lat_ref[...], rows, (((1,), (0,)), ((), ())), precision=HIGHEST, preferred_element_type=F32
        )


def finish(chi, lat, bands):
    return pl.pallas_call(
        finish_kernel,
        out_shape=jax.ShapeDtypeStruct(chi.shape, F32),
        compiler_params=params(),
    )(chi, lat, *bands)


def exchange(blocks, axis):
    return lax.all_to_all(blocks, axis, 0, 0, axis_index_groups=ALONG)


def to_all(block, axis):
    return exchange(jnp.broadcast_to(block[None], (4,) + block.shape), axis)


def both_of(x, step, axis):
    other = lax.ppermute(x, "lev", [(m, m ^ step) for m in range(8)])
    upper = (lax.axis_index("lev") // step) % 2
    return jnp.where(upper == 0, jnp.stack([x, other], axis), jnp.stack([other, x], axis))


def product(tiles, matrix):
    return jnp.einsum("yrc,ycd->rd", tiles, matrix, precision=HIGHEST, preferred_element_type=F32)


def shards(
    chi,
    mat_lon,
    mat_lat,
    mat_vert,
    chan_table,
    chan_map,
    error_weight,
    innovation,
    foot_weight,
    foot_slot,
    serve_cols,
):
    half = lax.axis_index("obs") % 2
    core = lax.axis_index("lat") % 2

    def near_far(x, axis, which):
        near = lax.dynamic_index_in_dim(x, which, axis, keepdims=False)
        far = lax.dynamic_index_in_dim(x, 1 - which, axis, keepdims=False)
        return near, far

    tile = (foot_slot >> 6) & 7
    slab = foot_slot >> 9
    group = 2 * ((tile & 1) ^ half) + (slab >> 2)
    place = (4 * group + (tile >> 1)) * BLOCK + (slab & 3) * CAP + (foot_slot & (CAP - 1))

    serve = serve_cols[0, 0].astype(F32).reshape(8, 4, 2, CAP).transpose(2, 1, 0, 3)
    near, far = near_far(serve, 0, half)
    half_piece = 2 * lax.axis_index("lat") + lax.axis_index("lev") % 2
    piece = lax.dynamic_index_in_dim(mat_lon.reshape(16, LANES, CELLS), half_piece, 0, keepdims=False)
    piece = jnp.concatenate([piece, far.reshape(8, CELLS)], axis=0)
    piece = lax.ppermute(piece, "obs", PARTNER)
    serve = jnp.stack([near, piece[LANES:].reshape(4, VIEWERS, CAP)], axis=1)
    serve = serve.reshape(4, 8, LANES)
    piece = both_of(piece[:LANES], 1, 0).reshape(CELLS, CELLS)
    band_near = to_all(chi, "lat")

    vertical = mat_vert.reshape(8 * LEVELS, 8, LEVELS)
    vertical = jnp.concatenate([vertical[:, :, :MAIN].reshape(8 * LEVELS, 8 * MAIN), vertical[:, :, MAIN]], axis=1)
    matches = (
        chan_map[:, None] == jnp.arange(chan_table.shape[0], dtype=jnp.int32)[None, :]
    ).astype(F32)
    selected = jnp.dot(matches, chan_table, precision=HIGHEST, preferred_element_type=F32)
    selected = jnp.dot(selected, vertical, precision=HIGHEST, preferred_element_type=F32)
    scaled = error_weight[:, None] * selected
    hessian = jnp.dot(selected.T, scaled, precision=HIGHEST, preferred_element_type=F32)
    constant = jnp.dot(scaled.T, innovation, precision=HIGHEST, preferred_element_type=F32)
    lats = near_far(mat_lat.reshape(16, 4, 2, 16), 2, core)
    lat_start = jnp.stack(lats, axis=1).reshape(16, 128)
    lat_finish = jnp.stack([m.reshape(16, 4, 2, 8).transpose(0, 2, 1, 3) for m in lats], axis=1).reshape(16, 128)
    band_near, serve, hessian, constant, lat_start, lat_finish = lax.optimization_barrier(
        (band_near, serve, hessian, constant, lat_start, lat_finish)
    )
    other_lon = lax.all_gather(piece, "lat", axis=0, tiled=False)
    lon_near, lon_far = near_far(mat_lon.reshape(4, 2, CELLS, CELLS), 1, half)
    other_near, other_far = near_far(other_lon.reshape(4, 2, CELLS, CELLS), 1, half)

    band_far = lax.ppermute(band_near, "lat", PARTNER)
    field, copies = start(lat_start, band_near, band_far, serve)
    other = lax.ppermute(field, "obs", PARTNER)
    near_tiles = exchange(copies, "obs")
    serve = near_tiles[:, HALVES * HALF :, :LANES]
    near_tiles = near_tiles[:, : HALVES * HALF]
    about = [x.reshape(LISTS, LANES) for x in (serve, place.astype(F32), foot_weight)]
    about = jnp.concatenate(about, axis=0)
    about, other = lax.optimization_barrier((about, other))
    far_tiles = to_all(other, "obs")
    about = both_of(about, 4, 0)
    about, far_tiles = lax.optimization_barrier((about, far_tiles))
    tile_near = product(near_tiles, lon_near) + product(far_tiles, lon_far)
    tile_far = product(near_tiles, other_near) + product(far_tiles, other_far)
    near_tiles = to_all(tile_near, "obs")
    about = both_of(about, 2, 1)
    about, near_tiles = lax.optimization_barrier((about, near_tiles))
    about = both_of(about, 1, 2).reshape(ABOUT)
    near = pick(near_tiles, about, 0)
    far = pick(to_all(tile_far, "obs"), about, 1)

    mean = lax.all_to_all(means(near, far, about), "lev", 0, 0)
    pulled = lax.all_to_all(pull(mean, hessian, constant), "lev", 0, 0)
    near, far = spread(pulled, about)

    far_tiles = exchange(add(exchange(put(far, about, 1), "obs")), "obs")
    near_tiles = exchange(add(exchange(put(near, about, 0), "obs")), "obs")
    far = product(far_tiles, other_far) + product(near_tiles, other_near)
    far = lax.ppermute(far, "obs", PARTNER)
    field = product(far_tiles, lon_far) + product(near_tiles, lon_near) + far
    band_near = to_all(field, "lat")
    band_far = lax.ppermute(band_near, "lat", PARTNER)
    return finish(chi, lat_finish, [band_near, band_far])


def solution(mesh):
    in_specs = (
        P("lev", "lat", "obs"),
        P(None, "obs"),
        P("lat", None),
        P(),
        P(),
        P(),
        P(),
        P(None, ("lat", "lev", "obs")),
        P(None, ("lat", "lev", "obs")),
        P(None, ("lat", "lev", "obs")),
        P("lat", ("lev", "obs"), None, None),
    )
    out_specs = P("lev", "lat", "obs")
    return jax.shard_map(shards, mesh=mesh, in_specs=in_specs, out_specs=out_specs, check_vma=False)
```

```python
import functools

import jax
import jax.numpy as jnp
from jax import lax
from jax.experimental import pallas as pl
from jax.experimental.pallas import tpu as pltpu
from jax.sharding import PartitionSpec as P

HIGHEST = lax.Precision.HIGHEST
F32 = jnp.float32
BF16 = jnp.bfloat16

LEVELS = 17
MAIN = 16
CELLS = 256
OWNER = 2 * MAIN
HALF = 4 * OWNER + 8
CAP = 64
VIEWERS = 8
OBS = 1024
FOOT = 4
BLOCK = 256
HALVES = 2
GROUP_MAIN = 4 * HALVES * MAIN
GROUP = GROUP_MAIN + 8
LANES = 128
LISTS = 32
COLUMN = MAIN * 8 + 8
PARTNER = [(t, t ^ 1) for t in range(8)]
ALONG = [[0, 2, 4, 6], [1, 3, 5, 7]]
VMEM = 48 * 1024 * 1024


def params():
    return pltpu.CompilerParams(vmem_limit_bytes=VMEM)


def split(x):
    high = x.astype(BF16)
    return high, (x - high.astype(F32)).astype(BF16)


def split_rows(x):
    return jnp.concatenate(split(x), axis=0)


def one_hot(index, rows):
    place = lax.broadcasted_iota(jnp.int32, (rows, index.shape[1]), 0)
    return jnp.where(place == index, 1.0, 0.0).astype(BF16)


def dot(a, b):
    return lax.dot_general(a, b, (((1,), (0,)), ((), ())), preferred_element_type=F32)


def dot_nt(a, b):
    return lax.dot_general(a, b, (((1,), (1,)), ((), ())), preferred_element_type=F32)


def lists_of(about_ref, tile, which):
    lists = []
    for slab in range(8):
        rows = about_ref[slab, pl.ds(pl.multiple_of(8 * tile, 8), 8), :]
        rows = [rows[4 * which + i : 4 * which + i + 1] for i in range(4)]
        lists.append(jnp.concatenate(rows, axis=1).astype(jnp.int32))
    return lists


def feet_of(about_ref, member, start):
    def row(first):
        at = first + 8 * member + start // LANES
        return jnp.concatenate([about_ref[0, at : at + 1, :], about_ref[0, at + 1 : at + 2, :]], axis=1)

    place = row(LISTS).astype(jnp.int32)
    return jnp.bitwise_and(place, BLOCK - 1), lax.shift_right_logical(place, 8), row(2 * LISTS)


def pick_kernel(which, field_ref, about_ref, slots_ref):
    tile = pl.program_id(0)
    lists = lists_of(about_ref, tile, which)
    for half in range(HALVES):
        base = half * HALF
        last = field_ref[0, base + 4 * OWNER : base + HALF, :]
        mains = []
        lasts = []
        for quarter in range(4):
            index = lists[4 * half + quarter]
            cell = jnp.bitwise_and(index, CELLS - 1)
            second = index >= CELLS
            start = base + quarter * OWNER
            rows = jnp.concatenate([field_ref[0, start : start + OWNER, :], last], axis=0)
            count = OWNER + 8
            both = dot(split_rows(rows), one_hot(cell, CELLS))
            picked = both[:count] + both[count:]
            mains.append(jnp.where(second, picked[MAIN:OWNER], picked[:MAIN]))
            at = OWNER + 2 * quarter
            lasts.append(jnp.where(second, picked[at + 1 : at + 2], picked[at : at + 1]))
        place = 4 * half + tile
        start = pl.multiple_of(place * MAIN, MAIN)
        for viewer in range(VIEWERS):
            lanes = slice(viewer * CAP, (viewer + 1) * CAP)
            slots_ref[viewer, pl.ds(start, MAIN), :] = jnp.concatenate([m[:, lanes] for m in mains], axis=1)
            slots_ref[viewer, pl.ds(GROUP_MAIN + place, 1), :] = jnp.concatenate([m[:, lanes] for m in lasts], axis=1)


ABOUT = (8, 3 * LISTS, LANES)


def pick(field, about, which):
    return pl.pallas_call(
        functools.partial(pick_kernel, which),
        grid=(4,),
        in_specs=[
            pl.BlockSpec((1, HALVES * HALF, CELLS), lambda y: (y, 0, 0)),
            pl.BlockSpec(ABOUT, lambda y: (0, 0, 0)),
        ],
        out_specs=pl.BlockSpec((VIEWERS, GROUP, BLOCK), lambda y: (0, 0, 0)),
        out_shape=jax.ShapeDtypeStruct((VIEWERS, GROUP, BLOCK), F32),
        compiler_params=params(),
    )(field, about)


def mean_kernel(about_ref, near_ref, far_ref, mean_ref):
    slots = near_ref, far_ref
    mains = jnp.concatenate([s[0, :GROUP_MAIN, :] for s in slots], axis=0)
    lasts = jnp.concatenate([s[0, GROUP_MAIN : GROUP_MAIN + 4 * HALVES, :] for s in slots], axis=0)
    values = split_rows(jnp.concatenate([mains, lasts], axis=0))
    total = 16 * MAIN + 16
    for start in range(0, OBS, BLOCK):
        main = jnp.zeros((MAIN, BLOCK), F32)
        last = jnp.zeros((16, BLOCK), F32)
        for member in range(FOOT):
            low, high, weight = feet_of(about_ref, member, start)
            both = dot(values, one_hot(low, BLOCK))
            picked = both[:total] + both[total:]
            masked = jnp.where(lax.broadcasted_iota(jnp.int32, (16, BLOCK), 0) == high, weight, 0.0)
            for part in range(16):
                main = main + picked[part * MAIN : (part + 1) * MAIN] * masked[part : part + 1]
            last = last + picked[16 * MAIN :] * masked
        last = jnp.sum(last, axis=0, keepdims=True)
        for piece in range(BLOCK // LANES):
            lanes = slice(piece * LANES, (piece + 1) * LANES)
            at = start // LANES + piece
            mean_ref[0, at * MAIN : (at + 1) * MAIN, :] = main[:, lanes]
            mean_ref[0, 8 * MAIN + at : 8 * MAIN + at + 1, :] = last[:, lanes]


def means(near, far, about):
    slots = pl.BlockSpec((1, GROUP, BLOCK), lambda v: (v, 0, 0))
    return pl.pallas_call(
        mean_kernel,
        grid=(VIEWERS,),
        in_specs=[pl.BlockSpec((1,) + ABOUT[1:], lambda v: (v, 0, 0)), slots, slots],
        out_specs=pl.BlockSpec((1, COLUMN, LANES), lambda v: (v, 0, 0)),
        out_shape=jax.ShapeDtypeStruct((VIEWERS, COLUMN, LANES), F32),
        compiler_params=params(),
    )(about, near, far)


def pull_kernel(mean_ref, hessian_ref, constant_ref, pulled_ref):
    columns = []
    for at in range(8):
        pieces = [mean_ref[m, at * MAIN : (at + 1) * MAIN, :] for m in range(8)]
        pieces += [mean_ref[m, 8 * MAIN + at : 8 * MAIN + at + 1, :] for m in range(8)]
        columns.append(jnp.concatenate(pieces, axis=0))
    pulled = lax.dot_general(
        hessian_ref[...],
        jnp.concatenate(columns, axis=1),
        (((1,), (0,)), ((), ())),
        precision=HIGHEST,
        preferred_element_type=F32,
    )
    pulled = pulled - constant_ref[...]
    for at in range(8):
        lanes = slice(at * LANES, (at + 1) * LANES)
        for m in range(8):
            pulled_ref[m, at * MAIN : (at + 1) * MAIN, :] = pulled[m * MAIN : (m + 1) * MAIN, lanes]
            pulled_ref[m, 8 * MAIN + at : 8 * MAIN + at + 1, :] = pulled[8 * MAIN + m : 8 * MAIN + m + 1, lanes]


def pull(mean, hessian, constant):
    return pl.pallas_call(
        pull_kernel,
        out_shape=jax.ShapeDtypeStruct((8, COLUMN, LANES), F32),
        compiler_params=params(),
    )(mean, hessian, constant)


def spread_kernel(grad_ref, about_ref, near_ref, far_ref):
    count = 16 * MAIN + 16
    total = jnp.zeros((2 * count, BLOCK), F32)
    for start in range(0, OBS, BLOCK):
        main = []
        last = []
        for at in range(start // LANES, (start + BLOCK) // LANES):
            main.append(grad_ref[0, at * MAIN : (at + 1) * MAIN, :])
            last.append(grad_ref[0, 8 * MAIN + at : 8 * MAIN + at + 1, :])
        main = jnp.concatenate(main, axis=1)
        last = jnp.concatenate(last, axis=1)
        for member in range(FOOT):
            low, high, weight = feet_of(about_ref, member, start)
            hit = jnp.where(lax.broadcasted_iota(jnp.int32, (16, BLOCK), 0) == high, 1.0, 0.0)
            main_high, main_low = split(main * weight)
            last_high, last_low = split(last * weight * hit)
            hits = [jnp.broadcast_to(hit[part : part + 1], (MAIN, BLOCK)).astype(BF16) for part in range(16)]
            rows = jnp.concatenate(
                [main_high * h for h in hits] + [last_high] + [main_low * h for h in hits] + [last_low], axis=0
            )
            total = total + dot_nt(rows, one_hot(low, BLOCK))
    total = total[:count] + total[count:]
    for group, slots_ref in enumerate((near_ref, far_ref)):
        slots_ref[0, :GROUP_MAIN, :] = total[group * GROUP_MAIN : (group + 1) * GROUP_MAIN]
        at = 16 * MAIN + group * 4 * HALVES
        slots_ref[0, GROUP_MAIN : GROUP_MAIN + 4 * HALVES, :] = total[at : at + 4 * HALVES]


def spread(grad, about):
    slots = pl.BlockSpec((1, GROUP, BLOCK), lambda v: (v, 0, 0))
    return pl.pallas_call(
        spread_kernel,
        grid=(VIEWERS,),
        in_specs=[
            pl.BlockSpec((1, COLUMN, LANES), lambda v: (v, 0, 0)),
            pl.BlockSpec((1,) + ABOUT[1:], lambda v: (v, 0, 0)),
        ],
        out_specs=[slots] * 2,
        out_shape=[jax.ShapeDtypeStruct((VIEWERS, GROUP, BLOCK), F32)] * 2,
        compiler_params=params(),
    )(grad, about)


def put_kernel(which, slots_ref, about_ref, field_ref):
    tile = pl.program_id(0)
    lists = lists_of(about_ref, tile, which)
    for half in range(HALVES):
        base = half * HALF
        place = 4 * half + tile
        start = pl.multiple_of(place * MAIN, MAIN)
        mains = [slots_ref[viewer, pl.ds(start, MAIN), :] for viewer in range(VIEWERS)]
        lasts = [slots_ref[viewer, pl.ds(GROUP_MAIN + place, 1), :] for viewer in range(VIEWERS)]
        tails = []
        for quarter in range(4):
            index = lists[4 * half + quarter]
            cell = jnp.bitwise_and(index, CELLS - 1)
            second = index >= CELLS
            lanes = slice(quarter * CAP, (quarter + 1) * CAP)
            main = jnp.concatenate([m[:, lanes] for m in mains], axis=1)
            last = jnp.concatenate([m[:, lanes] for m in lasts], axis=1)
            row = lax.broadcasted_iota(jnp.int32, (8, VIEWERS * CAP), 0)
            tail = jnp.where(row == jnp.where(second, 1, 0), last, 0.0)
            rows = jnp.concatenate([jnp.where(second, 0.0, main), jnp.where(second, main, 0.0), tail], axis=0)
            count = OWNER + 8
            both = dot_nt(split_rows(rows), one_hot(cell, CELLS))
            back = both[:count] + both[count:]
            field_ref[0, base + quarter * OWNER : base + (quarter + 1) * OWNER, :] = back[:OWNER]
            tails.append(back[OWNER : OWNER + 2])
        field_ref[0, base + 4 * OWNER : base + HALF, :] = jnp.concatenate(tails, axis=0)


def put(slots, about, which):
    return pl.pallas_call(
        functools.partial(put_kernel, which),
        grid=(4,),
        in_specs=[
            pl.BlockSpec((VIEWERS, GROUP, BLOCK), lambda y: (0, 0, 0)),
            pl.BlockSpec(ABOUT, lambda y: (0, 0, 0)),
        ],
        out_specs=pl.BlockSpec((1, HALVES * HALF, CELLS), lambda y: (y, 0, 0)),
        out_shape=jax.ShapeDtypeStruct((4, HALVES * HALF, CELLS), F32),
        compiler_params=params(),
    )(slots, about)


def add_kernel(parts_ref, sums_ref):
    total = parts_ref[0] + parts_ref[1] + parts_ref[2] + parts_ref[3]
    for copy in range(4):
        sums_ref[copy] = total


def add(parts):
    return pl.pallas_call(
        add_kernel, out_shape=jax.ShapeDtypeStruct(parts.shape, F32), compiler_params=params()
    )(parts)


def start_kernel(lat_ref, near_ref, far_ref, serve_ref, field_ref, copies_ref):
    size = HALVES * HALF
    copies_ref[:, size:, :LANES] = serve_ref[...]
    copies_ref[:, size:, LANES:] = jnp.zeros_like(serve_ref)
    levels = []
    for level in range(LEVELS):
        rows = jnp.concatenate([ref[x, level] for ref in (near_ref, far_ref) for x in range(4)], axis=0)
        levels.append(
            lax.dot_general(
                lat_ref[...], rows, (((1,), (0,)), ((), ())), precision=HIGHEST, preferred_element_type=F32
            )
        )
    main = jnp.swapaxes(jnp.stack(levels[:MAIN], axis=0), 0, 1)
    main = main.reshape(16 * MAIN, CELLS)
    for half in range(HALVES):
        rows = main[half * 8 * MAIN : (half + 1) * 8 * MAIN]
        last = levels[MAIN][8 * half : 8 * half + 8]
        base = half * HALF
        field_ref[base : base + 8 * MAIN, :] = rows
        field_ref[base + 8 * MAIN : base + HALF, :] = last
        for copy in range(4):
            copies_ref[copy, base : base + 8 * MAIN, :] = rows
            copies_ref[copy, base + 8 * MAIN : base + HALF, :] = last


def start(lat, near, far, serve):
    size = HALVES * HALF
    return pl.pallas_call(
        start_kernel,
        out_shape=[
            jax.ShapeDtypeStruct((size, CELLS), F32),
            jax.ShapeDtypeStruct((4, size + 8, CELLS), F32),
        ],
        compiler_params=params(),
    )(lat, near, far, serve)


def finish_kernel(chi_ref, lat_ref, *refs):
    bands, out_ref = refs[:-1], refs[-1]
    mains = []
    lasts = []
    for near_far in range(2):
        for half in range(2):
            ref = bands[near_far]
            base = half * HALF
            for x in range(4):
                main = ref[x, base : base + 4 * OWNER, :].reshape(8, MAIN, CELLS)
                mains.append(jnp.swapaxes(main, 0, 1))
                lasts.append(ref[x, base + 4 * OWNER : base + HALF, :])
    for level in range(LEVELS):
        rows = jnp.concatenate([m[level] for m in mains] if level < MAIN else lasts, axis=0)
        out_ref[level] = chi_ref[level] + lax.dot_general(
            lat_ref[...], rows, (((1,), (0,)), ((), ())), precision=HIGHEST, preferred_element_type=F32
        )


def finish(chi, lat, bands):
    return pl.pallas_call(
        finish_kernel,
        out_shape=jax.ShapeDtypeStruct(chi.shape, F32),
        compiler_params=params(),
    )(chi, lat, *bands)


def exchange(blocks, axis):
    return lax.all_to_all(blocks, axis, 0, 0, axis_index_groups=ALONG)


def to_all(block, axis):
    return exchange(jnp.broadcast_to(block[None], (4,) + block.shape), axis)


def both_of(x, step, axis):
    other = lax.ppermute(x, "lev", [(m, m ^ step) for m in range(8)])
    upper = (lax.axis_index("lev") // step) % 2
    return jnp.where(upper == 0, jnp.stack([x, other], axis), jnp.stack([other, x], axis))


def product(tiles, matrix):
    return jnp.einsum("yrc,ycd->rd", tiles, matrix, precision=lax.Precision.HIGH, preferred_element_type=F32)


def shards(
    chi,
    mat_lon,
    mat_lat,
    mat_vert,
    chan_table,
    chan_map,
    error_weight,
    innovation,
    foot_weight,
    foot_slot,
    serve_cols,
):
    half = lax.axis_index("obs") % 2
    core = lax.axis_index("lat") % 2

    def near_far(x, axis, which):
        near = lax.dynamic_index_in_dim(x, which, axis, keepdims=False)
        far = lax.dynamic_index_in_dim(x, 1 - which, axis, keepdims=False)
        return near, far

    tile = (foot_slot >> 6) & 7
    slab = foot_slot >> 9
    group = 2 * ((tile & 1) ^ half) + (slab >> 2)
    place = (4 * group + (tile >> 1)) * BLOCK + (slab & 3) * CAP + (foot_slot & (CAP - 1))

    serve = serve_cols[0, 0].astype(F32).reshape(8, 4, 2, CAP).transpose(2, 1, 0, 3)
    near, far = near_far(serve, 0, half)
    half_piece = 2 * lax.axis_index("lat") + lax.axis_index("lev") % 2
    piece = lax.dynamic_index_in_dim(mat_lon.reshape(16, LANES, CELLS), half_piece, 0, keepdims=False)
    piece = jnp.concatenate([piece, far.reshape(8, CELLS)], axis=0)
    piece = lax.ppermute(piece, "obs", PARTNER)
    serve = jnp.stack([near, piece[LANES:].reshape(4, VIEWERS, CAP)], axis=1)
    serve = serve.reshape(4, 8, LANES)
    band_near = to_all(chi, "lat")

    vertical = mat_vert.reshape(8 * LEVELS, 8, LEVELS)
    vertical = jnp.concatenate([vertical[:, :, :MAIN].reshape(8 * LEVELS, 8 * MAIN), vertical[:, :, MAIN]], axis=1)
    matches = (
        chan_map[:, None] == jnp.arange(chan_table.shape[0], dtype=jnp.int32)[None, :]
    ).astype(F32)
    selected = jnp.dot(matches, chan_table, precision=HIGHEST, preferred_element_type=F32)
    selected = jnp.dot(selected, vertical, precision=HIGHEST, preferred_element_type=F32)
    scaled = error_weight[:, None] * selected
    hessian = jnp.dot(selected.T, scaled, precision=HIGHEST, preferred_element_type=F32)
    constant = jnp.dot(scaled.T, innovation, precision=HIGHEST, preferred_element_type=F32)
    lats = near_far(mat_lat.reshape(16, 4, 2, 16), 2, core)
    lat_start = jnp.stack(lats, axis=1).reshape(16, 128)
    lat_finish = jnp.stack([m.reshape(16, 4, 2, 8).transpose(0, 2, 1, 3) for m in lats], axis=1).reshape(16, 128)
    band_near, serve, hessian, constant, lat_start, lat_finish = lax.optimization_barrier(
        (band_near, serve, hessian, constant, lat_start, lat_finish)
    )
    lon_near, lon_far = near_far(mat_lon.reshape(4, 2, CELLS, CELLS), 1, half)

    band_far = lax.ppermute(band_near, "lat", PARTNER)
    field, copies = start(lat_start, band_near, band_far, serve)
    other = lax.ppermute(field, "obs", PARTNER)
    near_tiles = exchange(copies, "obs")
    piece, near_tiles = lax.optimization_barrier((piece, near_tiles))
    piece = both_of(piece[:LANES], 1, 0).reshape(CELLS, CELLS)
    piece, other = lax.optimization_barrier((piece, other))
    other_lon = lax.all_gather(piece, "lat", axis=0, tiled=False)
    other_near, other_far = near_far(other_lon.reshape(4, 2, CELLS, CELLS), 1, half)
    serve = near_tiles[:, HALVES * HALF :, :LANES]
    near_tiles = near_tiles[:, : HALVES * HALF]
    about = [x.reshape(LISTS, LANES) for x in (serve, place.astype(F32), foot_weight)]
    about = jnp.concatenate(about, axis=0)
    about, other = lax.optimization_barrier((about, other))
    far_tiles = to_all(other, "obs")
    about = both_of(about, 4, 0)
    about, far_tiles = lax.optimization_barrier((about, far_tiles))
    tile_near = product(near_tiles, lon_near) + product(far_tiles, lon_far)
    tile_far = product(near_tiles, other_near) + product(far_tiles, other_far)
    near_tiles = to_all(tile_near, "obs")
    about = both_of(about, 2, 1)
    about = both_of(about, 1, 2).reshape(ABOUT)
    copies = jnp.broadcast_to(tile_far[None], (4,) + tile_far.shape)
    about, copies = lax.optimization_barrier((about, copies))
    near = pick(near_tiles, about, 0)
    far = pick(exchange(copies, "obs"), about, 1)

    mean = lax.all_to_all(means(near, far, about), "lev", 0, 0)
    pulled = lax.all_to_all(pull(mean, hessian, constant), "lev", 0, 0)
    near, far = spread(pulled, about)

    far_tiles = exchange(add(exchange(put(far, about, 1), "obs")), "obs")
    near_tiles = exchange(add(exchange(put(near, about, 0), "obs")), "obs")
    far = product(far_tiles, other_far) + product(near_tiles, other_near)
    far = lax.ppermute(far, "obs", PARTNER)
    field = product(far_tiles, lon_far) + product(near_tiles, lon_near) + far
    band_near = to_all(field, "lat")
    band_far = lax.ppermute(band_near, "lat", PARTNER)
    return finish(chi, lat_finish, [band_near, band_far])


def solution(mesh):
    in_specs = (
        P("lev", "lat", "obs"),
        P(None, "obs"),
        P("lat", None),
        P(),
        P(),
        P(),
        P(),
        P(None, ("lat", "lev", "obs")),
        P(None, ("lat", "lev", "obs")),
        P(None, ("lat", "lev", "obs")),
        P("lat", ("lev", "obs"), None, None),
    )
    out_specs = P("lev", "lat", "obs")
    return jax.shard_map(shards, mesh=mesh, in_specs=in_specs, out_specs=out_specs, check_vma=False)
```

```python
import functools

import jax
import jax.numpy as jnp
from jax import lax
from jax.experimental import pallas as pl
from jax.experimental.pallas import tpu as pltpu
from jax.sharding import PartitionSpec as P

HIGHEST = lax.Precision.HIGHEST
F32 = jnp.float32
BF16 = jnp.bfloat16

LEVELS = 17
MAIN = 16
CELLS = 256
OWNER = 2 * MAIN
HALF = 4 * OWNER + 8
CAP = 64
VIEWERS = 8
OBS = 1024
FOOT = 4
BLOCK = 256
HALVES = 2
GROUP_MAIN = 4 * HALVES * MAIN
GROUP = GROUP_MAIN + 8
LANES = 128
LISTS = 32
COLUMN = MAIN * 8 + 8
PARTNER = [(t, t ^ 1) for t in range(8)]
ALONG = [[0, 2, 4, 6], [1, 3, 5, 7]]
VMEM = 48 * 1024 * 1024


def params():
    return pltpu.CompilerParams(vmem_limit_bytes=VMEM)


def split(x):
    high = x.astype(BF16)
    return high, (x - high.astype(F32)).astype(BF16)


def split_rows(x):
    return jnp.concatenate(split(x), axis=0)


def one_hot(index, rows):
    place = lax.broadcasted_iota(jnp.int32, (rows, index.shape[1]), 0).astype(BF16)
    index = jnp.broadcast_to(index.astype(F32), place.shape).astype(BF16)
    return jnp.where(place == index, jnp.ones_like(place), jnp.zeros_like(place))


def dot(a, b):
    return lax.dot_general(a, b, (((1,), (0,)), ((), ())), preferred_element_type=F32)


def dot_nt(a, b):
    return lax.dot_general(a, b, (((1,), (1,)), ((), ())), preferred_element_type=F32)


def lists_of(about_ref, tile, which):
    lists = []
    for slab in range(8):
        rows = about_ref[slab, pl.ds(pl.multiple_of(8 * tile, 8), 8), :]
        rows = [rows[4 * which + i : 4 * which + i + 1] for i in range(4)]
        lists.append(jnp.concatenate(rows, axis=1).astype(jnp.int32))
    return lists


def feet_of(about_ref, member, start):
    def row(first):
        at = first + 8 * member + start // LANES
        return jnp.concatenate([about_ref[0, at : at + 1, :], about_ref[0, at + 1 : at + 2, :]], axis=1)

    place = row(LISTS).astype(jnp.int32)
    return jnp.bitwise_and(place, BLOCK - 1), lax.shift_right_logical(place, 8), row(2 * LISTS)


def pick_kernel(which, field_ref, about_ref, slots_ref):
    tile = pl.program_id(0)
    lists = lists_of(about_ref, tile, which)
    for half in range(HALVES):
        base = half * HALF
        last = field_ref[0, base + 4 * OWNER : base + HALF, :]
        mains = []
        lasts = []
        for quarter in range(4):
            index = lists[4 * half + quarter]
            cell = jnp.bitwise_and(index, CELLS - 1)
            second = index >= CELLS
            start = base + quarter * OWNER
            rows = jnp.concatenate([field_ref[0, start : start + OWNER, :], last], axis=0)
            count = OWNER + 8
            both = dot(split_rows(rows), one_hot(cell, CELLS))
            picked = both[:count] + both[count:]
            mains.append(jnp.where(second, picked[MAIN:OWNER], picked[:MAIN]))
            at = OWNER + 2 * quarter
            lasts.append(jnp.where(second, picked[at + 1 : at + 2], picked[at : at + 1]))
        place = 4 * half + tile
        start = pl.multiple_of(place * MAIN, MAIN)
        for viewer in range(VIEWERS):
            lanes = slice(viewer * CAP, (viewer + 1) * CAP)
            slots_ref[viewer, pl.ds(start, MAIN), :] = jnp.concatenate([m[:, lanes] for m in mains], axis=1)
            slots_ref[viewer, pl.ds(GROUP_MAIN + place, 1), :] = jnp.concatenate([m[:, lanes] for m in lasts], axis=1)


ABOUT = (8, 3 * LISTS, LANES)


def pick(field, about, which):
    return pl.pallas_call(
        functools.partial(pick_kernel, which),
        grid=(4,),
        in_specs=[
            pl.BlockSpec((1, HALVES * HALF, CELLS), lambda y: (y, 0, 0)),
            pl.BlockSpec(ABOUT, lambda y: (0, 0, 0)),
        ],
        out_specs=pl.BlockSpec((VIEWERS, GROUP, BLOCK), lambda y: (0, 0, 0)),
        out_shape=jax.ShapeDtypeStruct((VIEWERS, GROUP, BLOCK), F32),
        compiler_params=params(),
    )(field, about)


def mean_kernel(which, about_ref, slots_ref, *refs):
    before_ref, mean_ref = (None,) * (2 - len(refs)) + refs
    values = split_rows(slots_ref[0])
    for start in range(0, OBS, BLOCK):
        main = jnp.zeros((MAIN, BLOCK), F32)
        last = jnp.zeros((8, BLOCK), F32)
        for member in range(FOOT):
            low, high, weight = feet_of(about_ref, member, start)
            both = dot(values, one_hot(low, BLOCK))
            picked = both[:GROUP] + both[GROUP:]
            place = lax.broadcasted_iota(jnp.int32, (8, BLOCK), 0) + 8 * which
            masked = jnp.where(place == high, weight, 0.0)
            for part in range(8):
                main = main + picked[part * MAIN : (part + 1) * MAIN] * masked[part : part + 1]
            last = last + picked[GROUP_MAIN:] * masked
        last = jnp.sum(last, axis=0, keepdims=True)
        for piece in range(BLOCK // LANES):
            lanes = slice(piece * LANES, (piece + 1) * LANES)
            at = start // LANES + piece
            rows = slice(at * MAIN, (at + 1) * MAIN)
            row = slice(8 * MAIN + at, 8 * MAIN + at + 1)
            if before_ref is None:
                mean_ref[0, rows, :] = main[:, lanes]
                mean_ref[0, row, :] = last[:, lanes]
            else:
                mean_ref[0, rows, :] = before_ref[0, rows, :] + main[:, lanes]
                mean_ref[0, row, :] = before_ref[0, row, :] + last[:, lanes]


def means(slots, about, which, *before):
    column = pl.BlockSpec((1, COLUMN, LANES), lambda v: (v, 0, 0))
    return pl.pallas_call(
        functools.partial(mean_kernel, which),
        grid=(VIEWERS,),
        in_specs=[
            pl.BlockSpec((1,) + ABOUT[1:], lambda v: (v, 0, 0)),
            pl.BlockSpec((1, GROUP, BLOCK), lambda v: (v, 0, 0)),
        ]
        + [column] * len(before),
        out_specs=column,
        out_shape=jax.ShapeDtypeStruct((VIEWERS, COLUMN, LANES), F32),
        compiler_params=params(),
    )(about, slots, *before)


def pull_kernel(mean_ref, hessian_ref, constant_ref, pulled_ref):
    columns = []
    for at in range(8):
        pieces = [mean_ref[m, at * MAIN : (at + 1) * MAIN, :] for m in range(8)]
        pieces += [mean_ref[m, 8 * MAIN + at : 8 * MAIN + at + 1, :] for m in range(8)]
        columns.append(jnp.concatenate(pieces, axis=0))
    pulled = lax.dot_general(
        hessian_ref[...],
        jnp.concatenate(columns, axis=1),
        (((1,), (0,)), ((), ())),
        precision=HIGHEST,
        preferred_element_type=F32,
    )
    pulled = pulled - constant_ref[...]
    for at in range(8):
        lanes = slice(at * LANES, (at + 1) * LANES)
        for m in range(8):
            pulled_ref[m, at * MAIN : (at + 1) * MAIN, :] = pulled[m * MAIN : (m + 1) * MAIN, lanes]
            pulled_ref[m, 8 * MAIN + at : 8 * MAIN + at + 1, :] = pulled[8 * MAIN + m : 8 * MAIN + m + 1, lanes]


def pull(mean, hessian, constant):
    return pl.pallas_call(
        pull_kernel,
        out_shape=jax.ShapeDtypeStruct((8, COLUMN, LANES), F32),
        compiler_params=params(),
    )(mean, hessian, constant)


def spread_kernel(which, grad_ref, about_ref, slots_ref):
    total = jnp.zeros((2 * GROUP, BLOCK), F32)
    for start in range(0, OBS, BLOCK):
        main = []
        last = []
        for at in range(start // LANES, (start + BLOCK) // LANES):
            main.append(grad_ref[0, at * MAIN : (at + 1) * MAIN, :])
            last.append(grad_ref[0, 8 * MAIN + at : 8 * MAIN + at + 1, :])
        main = jnp.concatenate(main, axis=1)
        last = jnp.concatenate(last, axis=1)
        for member in range(FOOT):
            low, high, weight = feet_of(about_ref, member, start)
            place = lax.broadcasted_iota(jnp.int32, (8, BLOCK), 0) + 8 * which
            hit = jnp.where(place == high, 1.0, 0.0)
            main_high, main_low = split(main * weight)
            last_rows = last * weight * hit
            last_high = last_rows.astype(BF16).astype(F32)
            lasts = jnp.concatenate([last_high, last_rows - last_high], axis=0).astype(BF16)
            hits = [jnp.broadcast_to(hit[part : part + 1], (MAIN, BLOCK)).astype(BF16) for part in range(8)]
            rows = jnp.concatenate([main_high * h for h in hits] + [main_low * h for h in hits] + [lasts], axis=0)
            total = total + dot_nt(rows, one_hot(low, BLOCK))
    slots_ref[0, :GROUP_MAIN, :] = total[:GROUP_MAIN] + total[GROUP_MAIN : 2 * GROUP_MAIN]
    slots_ref[0, GROUP_MAIN:, :] = total[2 * GROUP_MAIN : 2 * GROUP_MAIN + 8] + total[2 * GROUP_MAIN + 8 :]


def spread(grad, about, which):
    return pl.pallas_call(
        functools.partial(spread_kernel, which),
        grid=(VIEWERS,),
        in_specs=[
            pl.BlockSpec((1, COLUMN, LANES), lambda v: (v, 0, 0)),
            pl.BlockSpec((1,) + ABOUT[1:], lambda v: (v, 0, 0)),
        ],
        out_specs=pl.BlockSpec((1, GROUP, BLOCK), lambda v: (v, 0, 0)),
        out_shape=jax.ShapeDtypeStruct((VIEWERS, GROUP, BLOCK), F32),
        compiler_params=params(),
    )(grad, about)


def put_kernel(which, slots_ref, about_ref, field_ref):
    tile = pl.program_id(0)
    lists = lists_of(about_ref, tile, which)
    for half in range(HALVES):
        base = half * HALF
        place = 4 * half + tile
        start = pl.multiple_of(place * MAIN, MAIN)
        mains = [slots_ref[viewer, pl.ds(start, MAIN), :] for viewer in range(VIEWERS)]
        lasts = [slots_ref[viewer, pl.ds(GROUP_MAIN + place, 1), :] for viewer in range(VIEWERS)]
        tails = []
        for quarter in range(4):
            index = lists[4 * half + quarter]
            cell = jnp.bitwise_and(index, CELLS - 1)
            second = index >= CELLS
            lanes = slice(quarter * CAP, (quarter + 1) * CAP)
            main = jnp.concatenate([m[:, lanes] for m in mains], axis=1)
            last = jnp.concatenate([m[:, lanes] for m in lasts], axis=1)
            row = lax.broadcasted_iota(jnp.int32, (8, VIEWERS * CAP), 0)
            tail = jnp.where(row == jnp.where(second, 1, 0), last, 0.0)
            rows = jnp.concatenate([jnp.where(second, 0.0, main), jnp.where(second, main, 0.0), tail], axis=0)
            count = OWNER + 8
            both = dot_nt(split_rows(rows), one_hot(cell, CELLS))
            back = both[:count] + both[count:]
            field_ref[0, base + quarter * OWNER : base + (quarter + 1) * OWNER, :] = back[:OWNER]
            tails.append(back[OWNER : OWNER + 2])
        field_ref[0, base + 4 * OWNER : base + HALF, :] = jnp.concatenate(tails, axis=0)


def put(slots, about, which):
    return pl.pallas_call(
        functools.partial(put_kernel, which),
        grid=(4,),
        in_specs=[
            pl.BlockSpec((VIEWERS, GROUP, BLOCK), lambda y: (0, 0, 0)),
            pl.BlockSpec(ABOUT, lambda y: (0, 0, 0)),
        ],
        out_specs=pl.BlockSpec((1, HALVES * HALF, CELLS), lambda y: (y, 0, 0)),
        out_shape=jax.ShapeDtypeStruct((4, HALVES * HALF, CELLS), F32),
        compiler_params=params(),
    )(slots, about)


def add_kernel(parts_ref, sums_ref):
    total = parts_ref[0] + parts_ref[1] + parts_ref[2] + parts_ref[3]
    for copy in range(4):
        sums_ref[copy] = total


def add(parts):
    return pl.pallas_call(
        add_kernel, out_shape=jax.ShapeDtypeStruct(parts.shape, F32), compiler_params=params()
    )(parts)


def start_kernel(lat_ref, near_ref, far_ref, serve_ref, field_ref, copies_ref):
    size = HALVES * HALF
    copies_ref[:, size:, :LANES] = serve_ref[...]
    copies_ref[:, size:, LANES:] = jnp.zeros_like(serve_ref)
    levels = []
    for level in range(LEVELS):
        rows = jnp.concatenate([ref[x, level] for ref in (near_ref, far_ref) for x in range(4)], axis=0)
        levels.append(
            lax.dot_general(
                lat_ref[...], rows, (((1,), (0,)), ((), ())), precision=HIGHEST, preferred_element_type=F32
            )
        )
    main = jnp.swapaxes(jnp.stack(levels[:MAIN], axis=0), 0, 1)
    main = main.reshape(16 * MAIN, CELLS)
    for half in range(HALVES):
        rows = main[half * 8 * MAIN : (half + 1) * 8 * MAIN]
        last = levels[MAIN][8 * half : 8 * half + 8]
        base = half * HALF
        field_ref[base : base + 8 * MAIN, :] = rows
        field_ref[base + 8 * MAIN : base + HALF, :] = last
        for copy in range(4):
            copies_ref[copy, base : base + 8 * MAIN, :] = rows
            copies_ref[copy, base + 8 * MAIN : base + HALF, :] = last


def start(lat, near, far, serve):
    size = HALVES * HALF
    return pl.pallas_call(
        start_kernel,
        out_shape=[
            jax.ShapeDtypeStruct((size, CELLS), F32),
            jax.ShapeDtypeStruct((4, size + 8, CELLS), F32),
        ],
        compiler_params=params(),
    )(lat, near, far, serve)


def finish_kernel(chi_ref, lat_ref, *refs):
    bands, out_ref = refs[:-1], refs[-1]
    mains = []
    lasts = []
    for near_far in range(2):
        for half in range(2):
            ref = bands[near_far]
            base = half * HALF
            for x in range(4):
                main = ref[x, base : base + 4 * OWNER, :].reshape(8, MAIN, CELLS)
                mains.append(jnp.swapaxes(main, 0, 1))
                lasts.append(ref[x, base + 4 * OWNER : base + HALF, :])
    for level in range(LEVELS):
        rows = jnp.concatenate([m[level] for m in mains] if level < MAIN else lasts, axis=0)
        out_ref[level] = chi_ref[level] + lax.dot_general(
            lat_ref[...], rows, (((1,), (0,)), ((), ())), precision=HIGHEST, preferred_element_type=F32
        )


def finish(chi, lat, bands):
    return pl.pallas_call(
        finish_kernel,
        out_shape=jax.ShapeDtypeStruct(chi.shape, F32),
        compiler_params=params(),
    )(chi, lat, *bands)


def exchange(blocks, axis):
    return lax.all_to_all(blocks, axis, 0, 0, axis_index_groups=ALONG)


def to_all(block, axis):
    return exchange(jnp.broadcast_to(block[None], (4,) + block.shape), axis)


def both_of(x, step, axis):
    other = lax.ppermute(x, "lev", [(m, m ^ step) for m in range(8)])
    upper = (lax.axis_index("lev") // step) % 2
    return jnp.where(upper == 0, jnp.stack([x, other], axis), jnp.stack([other, x], axis))


def product(tiles, matrix):
    return jnp.einsum("yrc,ycd->rd", tiles, matrix, precision=lax.Precision.HIGH, preferred_element_type=F32)


def shards(
    chi,
    mat_lon,
    mat_lat,
    mat_vert,
    chan_table,
    chan_map,
    error_weight,
    innovation,
    foot_weight,
    foot_slot,
    serve_cols,
):
    half = lax.axis_index("obs") % 2
    core = lax.axis_index("lat") % 2

    def near_far(x, axis, which):
        near = lax.dynamic_index_in_dim(x, which, axis, keepdims=False)
        far = lax.dynamic_index_in_dim(x, 1 - which, axis, keepdims=False)
        return near, far

    tile = (foot_slot >> 6) & 7
    slab = foot_slot >> 9
    group = 2 * ((tile & 1) ^ half) + (slab >> 2)
    place = (4 * group + (tile >> 1)) * BLOCK + (slab & 3) * CAP + (foot_slot & (CAP - 1))

    serve = serve_cols[0, 0].astype(F32).reshape(8, 4, 2, CAP).transpose(2, 1, 0, 3)
    near, far = near_far(serve, 0, half)
    half_piece = 2 * lax.axis_index("lat") + lax.axis_index("lev") % 2
    piece = lax.dynamic_index_in_dim(mat_lon.reshape(16, LANES, CELLS), half_piece, 0, keepdims=False)
    piece = jnp.concatenate([piece, far.reshape(8, CELLS)], axis=0)
    piece = lax.ppermute(piece, "obs", PARTNER)
    serve = jnp.stack([near, piece[LANES:].reshape(4, VIEWERS, CAP)], axis=1)
    serve = serve.reshape(4, 8, LANES)
    band_near = to_all(chi, "lat")

    vertical = mat_vert.reshape(8 * LEVELS, 8, LEVELS)
    vertical = jnp.concatenate([vertical[:, :, :MAIN].reshape(8 * LEVELS, 8 * MAIN), vertical[:, :, MAIN]], axis=1)
    matches = (
        chan_map[:, None] == jnp.arange(chan_table.shape[0], dtype=jnp.int32)[None, :]
    ).astype(F32)
    selected = jnp.dot(matches, chan_table, precision=HIGHEST, preferred_element_type=F32)
    selected = jnp.dot(selected, vertical, precision=HIGHEST, preferred_element_type=F32)
    scaled = error_weight[:, None] * selected
    hessian = jnp.dot(selected.T, scaled, precision=HIGHEST, preferred_element_type=F32)
    constant = jnp.dot(scaled.T, innovation, precision=HIGHEST, preferred_element_type=F32)
    lats = near_far(mat_lat.reshape(16, 4, 2, 16), 2, core)
    lat_start = jnp.stack(lats, axis=1).reshape(16, 128)
    lat_finish = jnp.stack([m.reshape(16, 4, 2, 8).transpose(0, 2, 1, 3) for m in lats], axis=1).reshape(16, 128)
    band_near, serve, hessian, constant, lat_start, lat_finish = lax.optimization_barrier(
        (band_near, serve, hessian, constant, lat_start, lat_finish)
    )
    lon_near, lon_far = near_far(mat_lon.reshape(4, 2, CELLS, CELLS), 1, half)

    band_far = lax.ppermute(band_near, "lat", PARTNER)
    field, copies = start(lat_start, band_near, band_far, serve)
    other = lax.ppermute(field, "obs", PARTNER)
    near_tiles = exchange(copies, "obs")
    piece, near_tiles = lax.optimization_barrier((piece, near_tiles))
    piece = both_of(piece[:LANES], 1, 0).reshape(CELLS, CELLS)
    piece, other = lax.optimization_barrier((piece, other))
    other_lon = lax.all_gather(piece, "lat", axis=0, tiled=False)
    other_near, other_far = near_far(other_lon.reshape(4, 2, CELLS, CELLS), 1, half)
    serve = near_tiles[:, HALVES * HALF :, :LANES]
    near_tiles = near_tiles[:, : HALVES * HALF]
    about = [x.reshape(LISTS, LANES) for x in (serve, place.astype(F32), foot_weight)]
    about = jnp.concatenate(about, axis=0)
    about, other = lax.optimization_barrier((about, other))
    far_tiles = to_all(other, "obs")
    about = both_of(about, 4, 0)
    about, far_tiles = lax.optimization_barrier((about, far_tiles))
    tile_near = product(near_tiles, lon_near) + product(far_tiles, lon_far)
    tile_far = product(near_tiles, other_near) + product(far_tiles, other_far)
    near_tiles = to_all(tile_near, "obs")
    about = both_of(about, 2, 1)
    about = both_of(about, 1, 2).reshape(ABOUT)
    copies = jnp.broadcast_to(tile_far[None], (4,) + tile_far.shape)
    about, copies = lax.optimization_barrier((about, copies))
    mean = means(pick(near_tiles, about, 0), about, 0)
    mean = means(pick(exchange(copies, "obs"), about, 1), about, 1, mean)

    mean = lax.all_to_all(mean, "lev", 0, 0)
    pulled = lax.all_to_all(pull(mean, hessian, constant), "lev", 0, 0)

    far_tiles = exchange(add(exchange(put(spread(pulled, about, 1), about, 1), "obs")), "obs")
    near_tiles = exchange(add(exchange(put(spread(pulled, about, 0), about, 0), "obs")), "obs")
    far = product(far_tiles, other_far) + product(near_tiles, other_near)
    far = lax.ppermute(far, "obs", PARTNER)
    field = product(far_tiles, lon_far) + product(near_tiles, lon_near) + far
    band_near = to_all(field, "lat")
    band_far = lax.ppermute(band_near, "lat", PARTNER)
    return finish(chi, lat_finish, [band_near, band_far])


def solution(mesh):
    in_specs = (
        P("lev", "lat", "obs"),
        P(None, "obs"),
        P("lat", None),
        P(),
        P(),
        P(),
        P(),
        P(None, ("lat", "lev", "obs")),
        P(None, ("lat", "lev", "obs")),
        P(None, ("lat", "lev", "obs")),
        P("lat", ("lev", "obs"), None, None),
    )
    out_specs = P("lev", "lat", "obs")
    return jax.shard_map(shards, mesh=mesh, in_specs=in_specs, out_specs=out_specs, check_vma=False)
```

```python
import functools

import jax
import jax.numpy as jnp
from jax import lax
from jax.experimental import pallas as pl
from jax.experimental.pallas import tpu as pltpu
from jax.sharding import PartitionSpec as P

HIGHEST = lax.Precision.HIGHEST
F32 = jnp.float32
BF16 = jnp.bfloat16

LEVELS = 17
MAIN = 16
CELLS = 256
OWNER = 2 * MAIN
HALF = 4 * OWNER + 8
CAP = 64
VIEWERS = 8
OBS = 1024
FOOT = 4
BLOCK = 256
HALVES = 2
GROUP_MAIN = 4 * HALVES * MAIN
GROUP = GROUP_MAIN + 8
LANES = 128
LISTS = 32
COLUMN = MAIN * 8 + 8
PARTNER = [(t, t ^ 1) for t in range(8)]
ALONG = [[0, 2, 4, 6], [1, 3, 5, 7]]
VMEM = 48 * 1024 * 1024


def params():
    return pltpu.CompilerParams(vmem_limit_bytes=VMEM)


def split(x):
    high = x.astype(BF16)
    return high, (x - high.astype(F32)).astype(BF16)


def split_rows(x):
    return jnp.concatenate(split(x), axis=0)


def one_hot(index, rows):
    place = lax.broadcasted_iota(jnp.int32, (rows, index.shape[1]), 0).astype(BF16)
    index = jnp.broadcast_to(index.astype(F32), place.shape).astype(BF16)
    return jnp.where(place == index, jnp.ones_like(place), jnp.zeros_like(place))


def dot(a, b):
    return lax.dot_general(a, b, (((1,), (0,)), ((), ())), preferred_element_type=F32)


def dot_nt(a, b):
    return lax.dot_general(a, b, (((1,), (1,)), ((), ())), preferred_element_type=F32)


def lists_of(about_ref, tile, which):
    lists = []
    for slab in range(8):
        rows = about_ref[slab, pl.ds(pl.multiple_of(8 * tile, 8), 8), :]
        rows = [rows[4 * which + i : 4 * which + i + 1] for i in range(4)]
        lists.append(jnp.concatenate(rows, axis=1).astype(jnp.int32))
    return lists


def feet_of(about_ref, member, start):
    def row(first):
        at = first + 8 * member + start // LANES
        return jnp.concatenate([about_ref[0, at : at + 1, :], about_ref[0, at + 1 : at + 2, :]], axis=1)

    place = row(LISTS).astype(jnp.int32)
    return jnp.bitwise_and(place, BLOCK - 1), lax.shift_right_logical(place, 8), row(2 * LISTS)


def pick_kernel(which, field_ref, about_ref, slots_ref):
    tile = pl.program_id(0)
    lists = lists_of(about_ref, tile, which)
    for half in range(HALVES):
        base = half * HALF
        last = field_ref[0, base + 4 * OWNER : base + HALF, :]
        mains = []
        lasts = []
        for quarter in range(4):
            index = lists[4 * half + quarter]
            cell = jnp.bitwise_and(index, CELLS - 1)
            second = index >= CELLS
            start = base + quarter * OWNER
            rows = jnp.concatenate([field_ref[0, start : start + OWNER, :], last], axis=0)
            count = OWNER + 8
            both = dot(split_rows(rows), one_hot(cell, CELLS))
            picked = both[:count] + both[count:]
            mains.append(jnp.where(second, picked[MAIN:OWNER], picked[:MAIN]))
            at = OWNER + 2 * quarter
            lasts.append(jnp.where(second, picked[at + 1 : at + 2], picked[at : at + 1]))
        place = 4 * half + tile
        start = pl.multiple_of(place * MAIN, MAIN)
        for viewer in range(VIEWERS):
            lanes = slice(viewer * CAP, (viewer + 1) * CAP)
            slots_ref[viewer, pl.ds(start, MAIN), :] = jnp.concatenate([m[:, lanes] for m in mains], axis=1)
            slots_ref[viewer, pl.ds(GROUP_MAIN + place, 1), :] = jnp.concatenate([m[:, lanes] for m in lasts], axis=1)


ABOUT = (8, 3 * LISTS, LANES)


def pick(field, about, which):
    return pl.pallas_call(
        functools.partial(pick_kernel, which),
        grid=(4,),
        in_specs=[
            pl.BlockSpec((1, HALVES * HALF, CELLS), lambda y: (y, 0, 0)),
            pl.BlockSpec(ABOUT, lambda y: (0, 0, 0)),
        ],
        out_specs=pl.BlockSpec((VIEWERS, GROUP, BLOCK), lambda y: (0, 0, 0)),
        out_shape=jax.ShapeDtypeStruct((VIEWERS, GROUP, BLOCK), F32),
        compiler_params=params(),
    )(field, about)


def mean_kernel(which, about_ref, slots_ref, *refs):
    before_ref, mean_ref = (None,) * (2 - len(refs)) + refs
    values = split_rows(slots_ref[0])
    for start in range(0, OBS, BLOCK):
        main = jnp.zeros((MAIN, BLOCK), F32)
        last = jnp.zeros((8, BLOCK), F32)
        for member in range(FOOT):
            low, high, weight = feet_of(about_ref, member, start)
            both = dot(values, one_hot(low, BLOCK))
            picked = both[:GROUP] + both[GROUP:]
            place = lax.broadcasted_iota(jnp.int32, (8, BLOCK), 0) + 8 * which
            masked = jnp.where(place == high, weight, 0.0)
            for part in range(8):
                main = main + picked[part * MAIN : (part + 1) * MAIN] * masked[part : part + 1]
            last = last + picked[GROUP_MAIN:] * masked
        last = jnp.sum(last, axis=0, keepdims=True)
        for piece in range(BLOCK // LANES):
            lanes = slice(piece * LANES, (piece + 1) * LANES)
            at = start // LANES + piece
            rows = slice(at * MAIN, (at + 1) * MAIN)
            row = slice(8 * MAIN + at, 8 * MAIN + at + 1)
            if before_ref is None:
                mean_ref[0, rows, :] = main[:, lanes]
                mean_ref[0, row, :] = last[:, lanes]
            else:
                mean_ref[0, rows, :] = before_ref[0, rows, :] + main[:, lanes]
                mean_ref[0, row, :] = before_ref[0, row, :] + last[:, lanes]


def means(slots, about, which, *before):
    column = pl.BlockSpec((1, COLUMN, LANES), lambda v: (v, 0, 0))
    return pl.pallas_call(
        functools.partial(mean_kernel, which),
        grid=(VIEWERS,),
        in_specs=[
            pl.BlockSpec((1,) + ABOUT[1:], lambda v: (v, 0, 0)),
            pl.BlockSpec((1, GROUP, BLOCK), lambda v: (v, 0, 0)),
        ]
        + [column] * len(before),
        out_specs=column,
        out_shape=jax.ShapeDtypeStruct((VIEWERS, COLUMN, LANES), F32),
        compiler_params=params(),
    )(about, slots, *before)


def pull_kernel(mean_ref, hessian_ref, constant_ref, pulled_ref):
    columns = []
    for at in range(8):
        pieces = [mean_ref[m, at * MAIN : (at + 1) * MAIN, :] for m in range(8)]
        pieces += [mean_ref[m, 8 * MAIN + at : 8 * MAIN + at + 1, :] for m in range(8)]
        columns.append(jnp.concatenate(pieces, axis=0))
    pulled = lax.dot_general(
        hessian_ref[...],
        jnp.concatenate(columns, axis=1),
        (((1,), (0,)), ((), ())),
        precision=HIGHEST,
        preferred_element_type=F32,
    )
    pulled = pulled - constant_ref[...]
    for at in range(8):
        lanes = slice(at * LANES, (at + 1) * LANES)
        for m in range(8):
            pulled_ref[m, at * MAIN : (at + 1) * MAIN, :] = pulled[m * MAIN : (m + 1) * MAIN, lanes]
            pulled_ref[m, 8 * MAIN + at : 8 * MAIN + at + 1, :] = pulled[8 * MAIN + m : 8 * MAIN + m + 1, lanes]


def pull(mean, hessian, constant):
    return pl.pallas_call(
        pull_kernel,
        out_shape=jax.ShapeDtypeStruct((8, COLUMN, LANES), F32),
        compiler_params=params(),
    )(mean, hessian, constant)


def spread_kernel(which, grad_ref, about_ref, slots_ref):
    total = jnp.zeros((2 * GROUP, BLOCK), F32)
    for start in range(0, OBS, BLOCK):
        main = []
        last = []
        for at in range(start // LANES, (start + BLOCK) // LANES):
            main.append(grad_ref[0, at * MAIN : (at + 1) * MAIN, :])
            last.append(grad_ref[0, 8 * MAIN + at : 8 * MAIN + at + 1, :])
        main = jnp.concatenate(main, axis=1)
        last = jnp.concatenate(last, axis=1)
        for member in range(FOOT):
            low, high, weight = feet_of(about_ref, member, start)
            place = lax.broadcasted_iota(jnp.int32, (8, BLOCK), 0) + 8 * which
            hit = jnp.where(place == high, 1.0, 0.0)
            main_high, main_low = split(main * weight)
            last_rows = last * weight * hit
            last_high = last_rows.astype(BF16).astype(F32)
            lasts = jnp.concatenate([last_high, last_rows - last_high], axis=0).astype(BF16)
            hits = [jnp.broadcast_to(hit[part : part + 1], (MAIN, BLOCK)).astype(BF16) for part in range(8)]
            rows = jnp.concatenate([main_high * h for h in hits] + [main_low * h for h in hits] + [lasts], axis=0)
            total = total + dot_nt(rows, one_hot(low, BLOCK))
    slots_ref[0, :GROUP_MAIN, :] = total[:GROUP_MAIN] + total[GROUP_MAIN : 2 * GROUP_MAIN]
    slots_ref[0, GROUP_MAIN:, :] = total[2 * GROUP_MAIN : 2 * GROUP_MAIN + 8] + total[2 * GROUP_MAIN + 8 :]


def spread(grad, about, which):
    return pl.pallas_call(
        functools.partial(spread_kernel, which),
        grid=(VIEWERS,),
        in_specs=[
            pl.BlockSpec((1, COLUMN, LANES), lambda v: (v, 0, 0)),
            pl.BlockSpec((1,) + ABOUT[1:], lambda v: (v, 0, 0)),
        ],
        out_specs=pl.BlockSpec((1, GROUP, BLOCK), lambda v: (v, 0, 0)),
        out_shape=jax.ShapeDtypeStruct((VIEWERS, GROUP, BLOCK), F32),
        compiler_params=params(),
    )(grad, about)


def put_kernel(which, slots_ref, about_ref, field_ref):
    tile = pl.program_id(0)
    lists = lists_of(about_ref, tile, which)
    for half in range(HALVES):
        base = half * HALF
        place = 4 * half + tile
        start = pl.multiple_of(place * MAIN, MAIN)
        mains = [slots_ref[viewer, pl.ds(start, MAIN), :] for viewer in range(VIEWERS)]
        lasts = [slots_ref[viewer, pl.ds(GROUP_MAIN + place, 1), :] for viewer in range(VIEWERS)]
        tails = []
        for quarter in range(4):
            index = lists[4 * half + quarter]
            cell = jnp.bitwise_and(index, CELLS - 1)
            second = index >= CELLS
            lanes = slice(quarter * CAP, (quarter + 1) * CAP)
            main = jnp.concatenate([m[:, lanes] for m in mains], axis=1)
            last = jnp.concatenate([m[:, lanes] for m in lasts], axis=1)
            row = lax.broadcasted_iota(jnp.int32, (8, VIEWERS * CAP), 0)
            tail = jnp.where(row == jnp.where(second, 1, 0), last, 0.0)
            rows = jnp.concatenate([jnp.where(second, 0.0, main), jnp.where(second, main, 0.0), tail], axis=0)
            count = OWNER + 8
            both = dot_nt(split_rows(rows), one_hot(cell, CELLS))
            back = both[:count] + both[count:]
            field_ref[0, base + quarter * OWNER : base + (quarter + 1) * OWNER, :] = back[:OWNER]
            tails.append(back[OWNER : OWNER + 2])
        field_ref[0, base + 4 * OWNER : base + HALF, :] = jnp.concatenate(tails, axis=0)


def put(slots, about, which):
    return pl.pallas_call(
        functools.partial(put_kernel, which),
        grid=(4,),
        in_specs=[
            pl.BlockSpec((VIEWERS, GROUP, BLOCK), lambda y: (0, 0, 0)),
            pl.BlockSpec(ABOUT, lambda y: (0, 0, 0)),
        ],
        out_specs=pl.BlockSpec((1, HALVES * HALF, CELLS), lambda y: (y, 0, 0)),
        out_shape=jax.ShapeDtypeStruct((4, HALVES * HALF, CELLS), F32),
        compiler_params=params(),
    )(slots, about)


def add_kernel(parts_ref, sums_ref):
    total = parts_ref[0] + parts_ref[1] + parts_ref[2] + parts_ref[3]
    for copy in range(4):
        sums_ref[copy] = total


def add(parts):
    return pl.pallas_call(
        add_kernel, out_shape=jax.ShapeDtypeStruct(parts.shape, F32), compiler_params=params()
    )(parts)


def start_kernel(lat_ref, near_ref, far_ref, serve_ref, field_ref, copies_ref):
    size = HALVES * HALF
    copies_ref[:, size:, :LANES] = serve_ref[...]
    copies_ref[:, size:, LANES:] = jnp.zeros_like(serve_ref)
    levels = []
    for level in range(LEVELS):
        rows = jnp.concatenate([ref[x, level] for ref in (near_ref, far_ref) for x in range(4)], axis=0)
        levels.append(
            lax.dot_general(
                lat_ref[...], rows, (((1,), (0,)), ((), ())), precision=HIGHEST, preferred_element_type=F32
            )
        )
    main = jnp.swapaxes(jnp.stack(levels[:MAIN], axis=0), 0, 1)
    main = main.reshape(16 * MAIN, CELLS)
    for half in range(HALVES):
        rows = main[half * 8 * MAIN : (half + 1) * 8 * MAIN]
        last = levels[MAIN][8 * half : 8 * half + 8]
        base = half * HALF
        field_ref[base : base + 8 * MAIN, :] = rows
        field_ref[base + 8 * MAIN : base + HALF, :] = last
        for copy in range(4):
            copies_ref[copy, base : base + 8 * MAIN, :] = rows
            copies_ref[copy, base + 8 * MAIN : base + HALF, :] = last


def start(lat, near, far, serve):
    size = HALVES * HALF
    return pl.pallas_call(
        start_kernel,
        out_shape=[
            jax.ShapeDtypeStruct((size, CELLS), F32),
            jax.ShapeDtypeStruct((4, size + 8, CELLS), F32),
        ],
        compiler_params=params(),
    )(lat, near, far, serve)


def finish_kernel(before_ref, lat_ref, band_ref, out_ref):
    mains = []
    lasts = []
    for half in range(2):
        base = half * HALF
        for x in range(4):
            main = band_ref[x, base : base + 4 * OWNER, :].reshape(8, MAIN, CELLS)
            mains.append(jnp.swapaxes(main, 0, 1))
            lasts.append(band_ref[x, base + 4 * OWNER : base + HALF, :])
    for level in range(LEVELS):
        rows = jnp.concatenate([m[level] for m in mains] if level < MAIN else lasts, axis=0)
        out_ref[level] = before_ref[level] + lax.dot_general(
            lat_ref[...], rows, (((1,), (0,)), ((), ())), precision=HIGHEST, preferred_element_type=F32
        )


def finish(before, lat, band):
    return pl.pallas_call(
        finish_kernel,
        out_shape=jax.ShapeDtypeStruct(before.shape, F32),
        compiler_params=params(),
    )(before, lat, band)


def exchange(blocks, axis):
    return lax.all_to_all(blocks, axis, 0, 0, axis_index_groups=ALONG)


def to_all(block, axis):
    return exchange(jnp.broadcast_to(block[None], (4,) + block.shape), axis)


def both_of(x, step, axis):
    other = lax.ppermute(x, "lev", [(m, m ^ step) for m in range(8)])
    upper = (lax.axis_index("lev") // step) % 2
    return jnp.where(upper == 0, jnp.stack([x, other], axis), jnp.stack([other, x], axis))


def product(tiles, matrix):
    return jnp.einsum("yrc,ycd->rd", tiles, matrix, precision=lax.Precision.HIGH, preferred_element_type=F32)


def shards(
    chi,
    mat_lon,
    mat_lat,
    mat_vert,
    chan_table,
    chan_map,
    error_weight,
    innovation,
    foot_weight,
    foot_slot,
    serve_cols,
):
    half = lax.axis_index("obs") % 2
    core = lax.axis_index("lat") % 2

    def near_far(x, axis, which):
        near = lax.dynamic_index_in_dim(x, which, axis, keepdims=False)
        far = lax.dynamic_index_in_dim(x, 1 - which, axis, keepdims=False)
        return near, far

    tile = (foot_slot >> 6) & 7
    slab = foot_slot >> 9
    group = 2 * ((tile & 1) ^ half) + (slab >> 2)
    place = (4 * group + (tile >> 1)) * BLOCK + (slab & 3) * CAP + (foot_slot & (CAP - 1))

    serve = serve_cols[0, 0].astype(F32).reshape(8, 4, 2, CAP).transpose(2, 1, 0, 3)
    near, far = near_far(serve, 0, half)
    half_piece = 2 * lax.axis_index("lat") + lax.axis_index("lev") % 2
    piece = lax.dynamic_index_in_dim(mat_lon.reshape(16, LANES, CELLS), half_piece, 0, keepdims=False)
    piece = jnp.concatenate([piece, far.reshape(8, CELLS)], axis=0)
    piece = lax.ppermute(piece, "obs", PARTNER)
    serve = jnp.stack([near, piece[LANES:].reshape(4, VIEWERS, CAP)], axis=1)
    serve = serve.reshape(4, 8, LANES)
    band_near = to_all(chi, "lat")

    vertical = mat_vert.reshape(8 * LEVELS, 8, LEVELS)
    vertical = jnp.concatenate([vertical[:, :, :MAIN].reshape(8 * LEVELS, 8 * MAIN), vertical[:, :, MAIN]], axis=1)
    matches = (
        chan_map[:, None] == jnp.arange(chan_table.shape[0], dtype=jnp.int32)[None, :]
    ).astype(F32)
    selected = jnp.dot(matches, chan_table, precision=HIGHEST, preferred_element_type=F32)
    selected = jnp.dot(selected, vertical, precision=HIGHEST, preferred_element_type=F32)
    scaled = error_weight[:, None] * selected
    hessian = jnp.dot(selected.T, scaled, precision=HIGHEST, preferred_element_type=F32)
    constant = jnp.dot(scaled.T, innovation, precision=HIGHEST, preferred_element_type=F32)
    lats = near_far(mat_lat.reshape(16, 4, 2, 16), 2, core)
    lat_start = jnp.stack(lats, axis=1).reshape(16, 128)
    lat_finish = [m.reshape(16, 4, 2, 8).transpose(0, 2, 1, 3).reshape(16, 64) for m in lats]
    band_near, serve, hessian, constant, lat_start, lat_finish = lax.optimization_barrier(
        (band_near, serve, hessian, constant, lat_start, lat_finish)
    )
    lon_near, lon_far = near_far(mat_lon.reshape(4, 2, CELLS, CELLS), 1, half)

    band_far = lax.ppermute(band_near, "lat", PARTNER)
    field, copies = start(lat_start, band_near, band_far, serve)
    other = lax.ppermute(field, "obs", PARTNER)
    near_tiles = exchange(copies, "obs")
    piece, near_tiles = lax.optimization_barrier((piece, near_tiles))
    piece = both_of(piece[:LANES], 1, 0).reshape(CELLS, CELLS)
    piece, other = lax.optimization_barrier((piece, other))
    other_lon = lax.all_gather(piece, "lat", axis=0, tiled=False)
    other_near, other_far = near_far(other_lon.reshape(4, 2, CELLS, CELLS), 1, half)
    serve = near_tiles[:, HALVES * HALF :, :LANES]
    near_tiles = near_tiles[:, : HALVES * HALF]
    about = [x.reshape(LISTS, LANES) for x in (serve, place.astype(F32), foot_weight)]
    about = jnp.concatenate(about, axis=0)
    about, other = lax.optimization_barrier((about, other))
    far_tiles = to_all(other, "obs")
    about = both_of(about, 4, 0)
    about, far_tiles = lax.optimization_barrier((about, far_tiles))
    tile_near = product(near_tiles, lon_near) + product(far_tiles, lon_far)
    tile_far = product(near_tiles, other_near)
    near_tiles = to_all(tile_near, "obs")
    about = both_of(about, 2, 1)
    about = both_of(about, 1, 2).reshape(ABOUT)
    about, tile_far = lax.optimization_barrier((about, tile_far))
    tile_far = tile_far + product(far_tiles, other_far)
    mean = means(pick(near_tiles, about, 0), about, 0)
    mean = means(pick(to_all(tile_far, "obs"), about, 1), about, 1, mean)

    mean = lax.all_to_all(mean, "lev", 0, 0)
    pulled = lax.all_to_all(pull(mean, hessian, constant), "lev", 0, 0)

    far_tiles = exchange(add(exchange(put(spread(pulled, about, 1), about, 1), "obs")), "obs")
    near_tiles = exchange(add(exchange(put(spread(pulled, about, 0), about, 0), "obs")), "obs")
    far = product(far_tiles, other_far) + product(near_tiles, other_near)
    far = lax.ppermute(far, "obs", PARTNER)
    field = product(far_tiles, lon_far) + product(near_tiles, lon_near) + far
    band_near = to_all(field, "lat")
    band_far = lax.ppermute(band_near, "lat", PARTNER)
    return finish(finish(chi, lat_finish[0], band_near), lat_finish[1], band_far)


def solution(mesh):
    in_specs = (
        P("lev", "lat", "obs"),
        P(None, "obs"),
        P("lat", None),
        P(),
        P(),
        P(),
        P(),
        P(None, ("lat", "lev", "obs")),
        P(None, ("lat", "lev", "obs")),
        P(None, ("lat", "lev", "obs")),
        P("lat", ("lev", "obs"), None, None),
    )
    out_specs = P("lev", "lat", "obs")
    return jax.shard_map(shards, mesh=mesh, in_specs=in_specs, out_specs=out_specs, check_vma=False)
```
